512 devices in a mesh: dp: 16 (over x, y), expert: 32 (over z, core).
Axes of the slice: x: 4, y: 4, z: 16, core: 2. Of those that a mesh axis runs over, the one named last changes fastest.
Arguments:
- grad_out: bfloat16 [4096, 4096], P('expert', 'dp'), may hold values from -12 to 12
- route_ids: int32 [4096, 8], P('expert'), may hold values from 0 to 63, all different within a row; in each aligned block of 128 rows (0 to 127, 128 to 255, ...) at most 17 rows name the same one
- route_weights: float32 [4096, 8], P('expert'), may hold values from 0.1 to 1
- hidden_act: bfloat16 [64, 544, 1536], P('expert', 'dp'), may hold values from -0.29882812 to 0.29882812
- down_weight: bfloat16 [64, 1536, 4096], P('expert', None, 'dp'), may hold values from -0.15625 to 0.15625
- skew_param: float32 [64, 24, 64, 64], P('expert'), may hold values from -0.12 to 0.12
Outputs:
- hidden_grad: bfloat16 [64, 544, 1536], P('expert', 'dp')
- skew_grad: float32 [64, 24, 64, 64], P('expert')
The draws below stay inside these ranges and needn't reach their ends.
Inputs may be any that keep to these rules, and one draw needn't show every extreme that they name: `route_ids`: each token names 8 different experts; within each aligned block of 128 tokens no expert is named by more than 17 of the block's choices, and in some block one expert is named by exactly 17.
All inputs are finite; a program needn't handle non-finite values.
Results may differ from the reference program's by a relative error of at most 0.02.
Values may be sent and summed in bfloat16 or wider, within the bound.
A program may use at most 128 MiB of HBM per device.

```python
import math
import jax
import jax.numpy as jnp
import numpy as np
from jax import lax

D = 4096
FF = 1536
TOP = 8
BS = 64
ORDER = 4
TOK_DEV = 128
EXPERTS = 64
TOKENS = 4096
NB = 24
FEAT = 256
MOST = 17
SLOTS = 544
N_DP = 16
N_EXPERT = 32


def steps_of(key, extent, pieces, smallest, top_value):
    def one(dim, parts):
        steps = jax.random.uniform(jax.random.fold_in(jax.random.fold_in(key, 6), dim), (parts,), jnp.float32, smallest / len(pieces), top_value / len(pieces))
        return jnp.repeat(jnp.exp(steps), extent[dim] // parts).reshape((-1,) + (1,) * (len(extent) - dim - 1))

    loudness = one(*pieces[0])
    for cut in pieces[1:]:
        loudness = loudness * one(*cut)
    return loudness


def routed_block(own_key, own, number, rows, number_of, top, reach, slope):
    ranking = jax.random.permutation(own_key, number_of)
    crowded, usual = shares(number_of, rows * top, reach, slope, True), shares(number_of, rows * top, reach, slope, False)
    places = jnp.arange(number_of)

    def named(tallies, turn):
        used = int((tallies > 0).sum())
        fixed = max(1, used // 4)
        passed = fixed + (places - fixed + turn * (used - fixed)) % max(1, number_of - fixed)
        return jnp.zeros((number_of,), jnp.int32).at[ranking[jnp.where(places < fixed, places, passed)]].set(jnp.asarray(tallies, jnp.int32))

    tallies = jnp.where(number % 4 == 0, named(crowded, number // 4), named(usual, number - number // 4 - 1))
    mixed = jax.random.permutation(jax.random.fold_in(own, 3), number_of)
    source_of, receiver = mixed[0:number_of // 2 * 2:2], mixed[1:number_of // 2 * 2:2]
    room = jnp.minimum(tallies[source_of] - 1, reach - tallies[receiver]) // 2
    room = jnp.where((source_of == ranking[0]) | (receiver == ranking[0]) | (tallies[receiver] == 0), 0, jnp.maximum(room, 0))
    passed = jax.random.randint(jax.random.fold_in(own, 4), (number_of // 2,), 0, 1 << 20) % (room + 1)
    tallies = tallies.at[source_of].add(-passed).at[receiver].add(passed)
    items = jnp.searchsorted(jnp.cumsum(tallies), jnp.arange(rows * top), side="right").astype(jnp.int32)
    table = items.reshape(top, rows).T
    table = table[jax.random.permutation(jax.random.fold_in(own, 1), rows)]
    turn = jax.random.randint(jax.random.fold_in(own, 2), (rows, 1), 0, top)
    return jnp.take_along_axis(table, (jnp.arange(top)[None, :] + turn) % top, axis=1)


def shares(count, total, bound, lean, full):
    portions = [(1 << 20) // math.isqrt(rank ** lean) + 1 for rank in range(1, count + 1)]
    largest = bound if full else min(bound, max(-(-total // count), total * portions[0] // sum(portions)))
    least = 1 if total - largest >= count - 1 else 0
    holding, rest = [largest] + [least] * (count - 1), total - largest - least * (count - 1)
    while rest > 0:
        candidates = [i for i in range(1, count) if holding[i] < largest] or [i for i in range(1, count) if holding[i] < bound]
        whole, left = sum([portions[i] for i in candidates]), rest
        for i in candidates:
            more = min(bound - holding[i], max(1, left * portions[i] // whole), rest)
            holding[i] = holding[i] + more
            rest = rest - more
    return np.array(holding)


def gaussian(key, dims, spread, reach, split=(), kind=jnp.bfloat16):
    result = spread * jax.random.normal(key, dims, jnp.float32)
    if split:
        result = result * steps_of(key, dims, split, -0.22, 0.18)
    return jnp.clip(result, -reach, reach).astype(kind)


def setup_inputs(seed: int = 0) -> dict:
    key_of = jax.random.split(jax.random.key(seed), 7)
    grad_out = gaussian(key_of[0], (TOKENS, D), 2.0, 12.0, ((0, 32), (1, 16)))
    route_ids_keys = jax.random.split(jax.random.fold_in(key_of[1], 1), TOKENS // TOK_DEV)
    route_ids_turns = jax.random.permutation(jax.random.fold_in(key_of[1], 3), TOKENS // TOK_DEV)
    route_ids = jax.vmap(lambda own, number: routed_block(jax.random.fold_in(key_of[1], 2), own, number, TOK_DEV, EXPERTS, TOP, MOST, 1))(route_ids_keys, route_ids_turns).reshape((TOKENS, TOP))
    route_weights = jnp.clip(jnp.exp(math.log(1.0) - 2.3025851 * jax.random.uniform(key_of[2], (TOKENS, TOP), jnp.float32) ** steps_of(key_of[2], (TOKENS, TOP), ((0, 32),), -0.2, 0.2)), 0.1, 1.0)
    hidden_act = gaussian(key_of[3], (EXPERTS, SLOTS, FF), 0.05, 0.29882812, ((0, 32), (1, 16)))
    down_weight = gaussian(key_of[4], (EXPERTS, FF, D), FF ** -0.5, 0.15625, ((0, 32), (2, 16)))
    skew_param = gaussian(key_of[5], (EXPERTS, NB, BS, BS), 0.02, 0.12, ((0, 32),), jnp.float32)
    return dict(grad_out=grad_out, route_ids=route_ids, route_weights=route_weights, hidden_act=hidden_act, down_weight=down_weight, skew_param=skew_param)


def rotation(skew_param):
    skew_mat = skew_param - jnp.swapaxes(skew_param, -1, -2)
    identity = jnp.eye(skew_mat.shape[-1], dtype=jnp.float32)
    negated = -skew_mat
    series = identity + negated
    powered = negated
    for factor_step in range(1, ORDER):
        powered = jnp.einsum('...ij,...jk->...ik', powered, powered, precision=lax.Precision.HIGHEST)
        series = jnp.einsum('...ij,...jk->...ik', series, identity + powered, precision=lax.Precision.HIGHEST)
    return jnp.einsum('...ij,...jk->...ik', identity - skew_mat, series, precision=lax.Precision.HIGHEST)

def expert_rows(operands):
    routed_rows, weight_rows = operands
    summed = jnp.zeros((SLOTS, FF), jnp.float32)
    for group in range(N_DP):
        segment = routed_rows[:, group * FEAT:(group + 1) * FEAT]
        weights = weight_rows[:, group * FEAT:(group + 1) * FEAT]
        partial_sum = jnp.dot(segment, weights.T, preferred_element_type=jnp.float32).astype(jnp.bfloat16)
        partial_sum = lax.optimization_barrier(partial_sum)
        summed = summed + partial_sum.astype(jnp.float32)
    return summed

def reference(grad_out, route_ids, route_weights, hidden_act, down_weight, skew_param):
    flat_ids = route_ids.reshape(-1).astype(jnp.int32)
    onehot = (flat_ids[:, None] == jnp.arange(EXPERTS, dtype=jnp.int32)[None, :]).astype(jnp.int32)
    blocked = onehot.reshape(N_EXPERT, TOK_DEV * TOP, EXPERTS)
    before = jnp.cumsum(blocked, axis=1) - blocked
    position = lax.optimization_barrier(jnp.sum(before * blocked, axis=2)).reshape(-1)
    block_ids = (jnp.arange(TOKENS * TOP, dtype=jnp.int32) // (TOK_DEV * TOP)).astype(jnp.int32)
    slot_index = (flat_ids * SLOTS + block_ids * MOST + position).astype(jnp.int32)
    sent_rows = (route_weights[:, :, None] * grad_out[:, None, :].astype(jnp.float32)).astype(jnp.bfloat16)
    sent_rows = sent_rows.reshape(TOKENS * TOP, D)
    routed = jnp.zeros((EXPERTS * SLOTS, D), jnp.bfloat16).at[slot_index].set(sent_rows)
    routed = routed.reshape(EXPERTS, SLOTS, D)
    row_grad = lax.map(expert_rows, (routed, down_weight))
    rotated, pullback = jax.vjp(rotation, skew_param)
    grad_blocks = row_grad.reshape(EXPERTS, SLOTS, NB, BS)
    hidden_grad = jnp.einsum('esbc,ebac->esba', grad_blocks, rotated, precision=lax.Precision.HIGHEST)
    hidden_grad = hidden_grad.astype(jnp.bfloat16).reshape(EXPERTS, SLOTS, FF)
    act_blocks = hidden_act.astype(jnp.float32).reshape(EXPERTS, SLOTS, NB, BS)
    rot_grad = jnp.einsum('esba,esbc->ebac', act_blocks, grad_blocks, precision=lax.Precision.HIGHEST)
    skew_grad = pullback(rot_grad)[0]
    return (hidden_grad, skew_grad)
```

```python
import functools

import jax
import jax.numpy as jnp
from jax import lax
from jax.experimental import pallas as pl
from jax.experimental.pallas import tpu as pltpu
from jax.sharding import PartitionSpec as P

F32 = jnp.float32
BF16 = jnp.bfloat16
MESH = pl.DeviceIdType.MESH
MOST = 17
PER = 4
HEAD = 40
DEEP = 48


def dot(a, b, dims=((1,), (0,))):
    return lax.dot_general(a, b, (dims, ((), ())), preferred_element_type=F32)


def halves(value):
    high = value.astype(BF16)
    return high, (value - high.astype(F32)).astype(BF16)


def spread(slab, mask):
    return jnp.concatenate([slab] * PER, axis=0) * mask


def fold(square):
    size = square.shape[0] // PER
    total = square[:size]
    for band in range(1, PER):
        total = total + square[band * size : (band + 1) * size]
    return total


def both(slab, mask):
    high, low = halves(slab)
    return spread(high, mask), spread(low, mask)


def times(left, right):
    rows = left.shape[0]
    high, low = halves(left)
    first = dot(jnp.concatenate([high, low], axis=0), right[0])
    return first[:rows] + first[rows:] + dot(high, right[1])


def negated_skew(stack, mask):
    square = spread(stack.T, mask)
    return fold(square - square.T)


def kernel(
    side, depth, groups,
    ids_ref, wts_ref, grad_ref, act_ref, w_ref, skew_ref,
    hid_ref, skg_ref,
    gath, part, rxa, rxb, mida, midb, tra, trb, rgs, rotm, rotp, rotrx, pull, maskf, maskb, bys, lefts, values,
    s_right, s_left, s_sib, r_gath, s_a, s_b, r_a, r_b, s_ma, s_mb, r_ma, r_mb,
    s_rot, r_rot, s_pull, r_pull,
):
    n_dp = side * side
    dp = lax.axis_index("dp")
    ex = lax.axis_index("expert")
    x, y = dp // side, dp % side
    z, core = ex // 2, ex % 2
    hidden = w_ref.shape[1]
    half = hidden // 2
    size = skew_ref.shape[1] // PER
    per_expert = groups // 2
    right = lax.rem(z + 1, depth) * 2 + core
    left = lax.rem(z + depth - 1, depth) * 2 + core
    sibling = z * 2 + (1 - core)

    def copy(src, dst, send, recv, to_dp, to_ex):
        return pltpu.make_async_remote_copy(
            src_ref=src, dst_ref=dst, send_sem=send, recv_sem=recv,
            device_id=(to_dp, to_ex), device_id_type=MESH,
        )

    barrier = pltpu.get_barrier_semaphore()
    for peer in (right, left, sibling):
        pl.semaphore_signal(barrier, inc=1, device_id=(dp, peer), device_id_type=MESH)

    def greet(step, carry):
        pl.semaphore_signal(
            barrier, inc=1, device_id=(lax.rem(dp + step, n_dp), ex), device_id_type=MESH
        )
        return carry

    lax.fori_loop(1, n_dp, greet, 0)

    tokens = grad_ref.shape[0]
    own = ex
    gath[own, 0:tokens, :] = grad_ref[...]
    weight = wts_ref[...]
    w1 = weight.astype(BF16).astype(F32)
    w2 = (weight - w1).astype(BF16).astype(F32)
    w3 = weight - w1 - w2
    info = jnp.concatenate(
        [
            jnp.concatenate([ids_ref[...].astype(F32), w1], axis=1),
            jnp.concatenate([w2, w3], axis=1),
        ],
        axis=0,
    )
    gath[own, tokens : tokens + 16, :] = info.astype(BF16)

    row_i = lax.broadcasted_iota(jnp.int32, (PER * size, PER * size), 0) // size
    col_i = lax.broadcasted_iota(jnp.int32, (PER * size, PER * size), 1) // size
    maskf[...] = (row_i == col_i).astype(F32)
    maskb[...] = (row_i == col_i).astype(F32).astype(BF16)

    pl.semaphore_wait(barrier, n_dp - 1 + 3)

    def go_right(block):
        return copy(gath.at[block], gath.at[block], s_right.at[block // 2], r_gath.at[block], dp, right)

    def go_left(block):
        return copy(gath.at[block], gath.at[block], s_left.at[block // 2], r_gath.at[block], dp, left)

    def go_across(block):
        return copy(gath.at[block], gath.at[block], s_sib.at[block // 2], r_gath.at[block], dp, sibling)

    go_right(own).start()
    go_left(own).start()
    go_across(own).start()

    upper = (
        lax.broadcasted_iota(jnp.int32, (tokens, tokens), 0)
        < lax.broadcasted_iota(jnp.int32, (tokens, tokens), 1)
    ).astype(F32).astype(BF16)

    def rows_of(root):
        hits, heavy = [], []
        for turn in range(2):
            data = gath[root * 2 + turn, tokens : tokens + 16, :].astype(F32)
            named = data[0:8, 0:tokens]
            weights = data[0:8, tokens:] + data[8:16, 0:tokens] + data[8:16, tokens:]
            for local in range(2):
                hit = (named == (ex * 2 + local).astype(F32)).astype(F32)
                hits.append(jnp.sum(hit, axis=0, keepdims=True))
                heavy.append(jnp.sum(hit * weights, axis=0, keepdims=True))
        taken = jnp.concatenate(hits + [jnp.zeros((4, tokens), F32)], axis=0)
        rank = dot(taken.astype(BF16), upper)
        place = lax.broadcasted_iota(jnp.int32, (HEAD, tokens), 0).astype(F32)
        picks, scales = [], []
        for local in range(2):
            chosen, scale = [], None
            for turn in range(2):
                at = turn * 2 + local
                slot = jnp.where(
                    taken[at : at + 1] > 0, rank[at : at + 1] + float(turn * MOST), -1.0
                )
                equal = place == slot
                chosen.append(equal.astype(F32))
                term = jnp.sum(jnp.where(equal, heavy[at], 0.0), axis=1, keepdims=True)
                scale = term if scale is None else scale + term
            picks.append(jnp.concatenate(chosen, axis=1))
            scales.append(scale)
        pick = jnp.concatenate(picks, axis=0).astype(BF16)
        rows = jnp.concatenate(
            [gath[root * 2, 0:tokens, :], gath[root * 2 + 1, 0:tokens, :]], axis=0
        )
        routed = dot(pick, rows)
        return [routed[local * HEAD : (local + 1) * HEAD] * scales[local] for local in range(2)]

    def process(roots):
        found = [rows_of(root) for root in roots]
        sums = []
        for local in range(2):
            lhs = jnp.concatenate([f[local] for f in found], axis=0).astype(BF16)
            sums.append(dot(lhs, w_ref[local], ((1,), (1,))))
        for n, root in enumerate(roots):
            for which in range(2):
                part[root, which] = jnp.concatenate(
                    [
                        s[n * HEAD : (n + 1) * HEAD, which * half : (which + 1) * half]
                        for s in sums
                    ],
                    axis=0,
                ).astype(BF16)
            jx, jy = root // side, root % side

            @pl.when(jy != y)
            def _():
                first_a(root).start()

            @pl.when(jx != x)
            def _():
                first_b(root).start()

    def first_a(root):
        jx, jy = root // side, root % side
        off = lax.rem(jy - y + side, side)
        slot = jnp.maximum(off - 1, 0)
        return copy(part.at[root, 0], rxa.at[jx, slot], s_a.at[root], r_a.at[jx, slot], x * side + jy, ex)

    def first_b(root):
        jx, jy = root // side, root % side
        off = lax.rem(jx - x + side, side)
        slot = jnp.maximum(off - 1, 0)
        return copy(part.at[root, 1], rxb.at[jy, slot], s_b.at[root], r_b.at[jy, slot], jx * side + y, ex)

    def arrived(block):
        go_right(block).wait_recv()

    arrived(sibling)
    process([z])

    def ring(step, carry):
        low = lax.rem(z - step + depth, depth)
        high = lax.rem(z + step, depth)
        arrived(low * 2 + core)
        go_right(low * 2 + core).start()
        arrived(high * 2 + core)

        @pl.when(step < depth // 2 - 1)
        def _():
            go_left(high * 2 + core).start()

        go_across(low * 2 + core).start()
        go_across(high * 2 + core).start()
        arrived(low * 2 + 1 - core)
        arrived(high * 2 + 1 - core)
        process([low, high])
        return carry

    lax.fori_loop(1, depth // 2, ring, 0)
    far = lax.rem(z + depth // 2, depth)
    arrived(far * 2 + core)
    go_across(far * 2 + core).start()
    arrived(far * 2 + 1 - core)
    process([far])

    eye = (
        lax.broadcasted_iota(jnp.int32, (size, PER * size), 0)
        == lax.rem(lax.broadcasted_iota(jnp.int32, (size, PER * size), 1), size)
    ).astype(F32)

    def turn(group, carry):
        mask = maskb[...]
        first = negated_skew(skew_ref[group], maskf[...])
        by_first = both(first, mask)
        second = times(first, by_first)
        series = eye + first
        pair = times(jnp.concatenate([second, series], axis=0), both(second, mask))
        fourth, series = pair[:size], series + pair[size:]
        pair = times(jnp.concatenate([fourth, series], axis=0), both(fourth, mask))
        eighth, series = pair[:size], series + pair[size:]
        series = series + times(series, both(eighth, mask))
        result = series + times(series, by_first)
        rotm[group] = spread(result.astype(BF16), mask)
        return carry

    lax.fori_loop(0, groups, turn, 0)

    def prepare():
        mask = maskb[...]
        given = -negated_skew(skew_ref[jnp.minimum(dp, groups - 1)], maskf[...])

        def keep(which, slab):
            right = both(slab, mask)
            bys[which] = right[0]
            return right

        second = times(given, keep(0, given))
        one = eye + given
        pair = times(jnp.concatenate([second, one], axis=0), keep(1, second))
        fourth, two = pair[:size], one + pair[size:]
        pair = times(jnp.concatenate([fourth, two], axis=0), keep(2, fourth))
        eighth, three = pair[:size], two + pair[size:]
        keep(4, three + times(three, keep(3, eighth)))
        for which, slab in enumerate((given, second, one, fourth, two, three)):
            lefts[which] = slab.astype(BF16)

    prepare()

    def gather_a(jx, carry):
        root = jx * side + y
        total = part[root, 0].astype(F32)
        for slot in range(side - 1):
            copy(part.at[root, 0], rxa.at[jx, slot], s_a.at[root], r_a.at[jx, slot], dp, ex).wait_recv()
            total = total + rxa[jx, slot].astype(F32)
        mida[jx] = total.astype(BF16)

        @pl.when(jx != x)
        def _():
            second_a(jx).start()

        return carry

    def second_a(jx):
        slot = jnp.maximum(lax.rem(jx - x + side, side) - 1, 0)
        return copy(mida.at[jx], tra.at[slot], s_ma.at[jx], r_ma.at[slot], jx * side + y, ex)

    def gather_b(jy, carry):
        root = x * side + jy
        total = part[root, 1].astype(F32)
        for slot in range(side - 1):
            copy(part.at[root, 1], rxb.at[jy, slot], s_b.at[root], r_b.at[jy, slot], dp, ex).wait_recv()
            total = total + rxb[jy, slot].astype(F32)
        midb[jy] = total.astype(BF16)

        @pl.when(jy != y)
        def _():
            second_b(jy).start()

        return carry

    def second_b(jy):
        slot = jnp.maximum(lax.rem(jy - y + side, side) - 1, 0)
        return copy(midb.at[jy], trb.at[slot], s_mb.at[jy], r_mb.at[slot], x * side + jy, ex)

    def gather_both(step, carry):
        gather_a(step, 0)
        gather_b(step, 0)
        return carry

    lax.fori_loop(0, side, gather_both, 0)

    for which, (mid, at, tr, s_m, r_m) in enumerate(((mida, x, tra, s_ma, r_ma), (midb, y, trb, s_mb, r_mb))):
        total = mid[at].astype(F32)
        for slot in range(side - 1):
            copy(mid.at[0], tr.at[slot], s_m.at[0], r_m.at[slot], dp, ex).wait_recv()
            total = total + tr[slot].astype(F32)
        for local in range(2):
            rgs[local, :, which * half : (which + 1) * half] = jnp.concatenate(
                [total[local * HEAD : (local + 1) * HEAD], jnp.zeros((DEEP - HEAD, half), F32)], axis=0
            ).astype(BF16)

    def lanes_of(group):
        return pl.ds(pl.multiple_of((group % per_expert) * PER * size, PER * size), PER * size)

    def rot_copy(group):
        return copy(rotp.at[group], rotrx.at[dp], s_rot.at[group], r_rot.at[dp], group, ex)

    def grads(group, carry):
        local, lanes = group // per_expert, lanes_of(group)
        square = dot(act_ref[local, :, lanes], rgs[local, :, lanes], ((0,), (0,)))
        rotp[group] = fold(square * maskf[...]).astype(BF16)

        @pl.when(group != dp)
        def _():
            rot_copy(group).start()

        return carry

    lax.fori_loop(0, groups, grads, 0)

    def hide(group, carry):
        local, lanes = group // per_expert, lanes_of(group)
        hid_ref[local, :, lanes] = dot(rgs[local, :, lanes], rotm[group], ((1,), (1,))).astype(BF16)
        return carry

    lax.fori_loop(0, groups, hide, 0)

    def pull_copy(owner, peer):
        return copy(pull.at[owner], pull.at[owner], s_pull.at[peer], r_pull.at[owner], peer, ex)

    @pl.when(dp < groups)
    def _():
        mask = maskb[...]

        def add(step, total):
            source = lax.rem(dp + step, n_dp)
            copy(rotp.at[0], rotrx.at[source], s_rot.at[0], r_rot.at[source], dp, ex).wait_recv()
            return total + rotrx[source].astype(F32)

        change = lax.fori_loop(1, n_dp, add, rotp[dp].astype(F32))
        change_b = change.astype(BF16)

        none = dp // n_dp

        def put(at, left, right):
            rows = left.shape[0] // size
            values[at : at + rows] = dot(left, right).reshape(rows, size, PER * size)
            return [values[at + row + none] for row in range(rows)]

        def rows_at(first, count):
            return lefts[first : first + count].reshape(count * size, PER * size)

        (front,) = put(0, rows_at(0, 1), spread(change_b, mask))
        (back,) = put(1, change_b, bys[0])
        change2 = (front + back).astype(BF16)
        front, lower = put(2, rows_at(1, 2), spread(change2, mask))
        (back,) = put(4, change2, bys[1])
        change4 = (front + back).astype(BF16)
        (back,) = put(5, change_b, bys[1])
        two_change = change + back + lower
        front, lower = put(6, rows_at(3, 2), spread(change4, mask))
        (back,) = put(8, change4, bys[2])
        change8 = (front + back).astype(BF16)
        (back,) = put(9, two_change.astype(BF16), bys[2])
        three_change = two_change + back + lower
        (lower,) = put(10, rows_at(5, 1), spread(change8, mask))
        (back,) = put(11, three_change.astype(BF16), bys[3])
        four_change = three_change + back + lower
        (front,) = put(12, rows_at(0, 1), spread(four_change.astype(BF16), mask))
        (back,) = put(13, change_b, bys[4])
        result = front + four_change + back
        square = spread(result, maskf[...])
        pull[dp] = fold(square.T - square).astype(BF16)

        def tell(step, carry):
            pull_copy(dp, lax.rem(dp + step, n_dp)).start()
            return carry

        lax.fori_loop(1, n_dp, tell, 0)

    def write(group, carry):
        @pl.when(group != dp)
        def _():
            pull_copy(group, dp).wait_recv()

        skg_ref[group] = -(pull[group].astype(F32).T)
        return carry

    lax.fori_loop(0, groups, write, 0)

    def left_ring(step, carry):
        go_across(lax.rem(z + step, depth) * 2 + core).wait_send()

        @pl.when(step < depth // 2)
        def _():
            go_right(lax.rem(z - step + depth, depth) * 2 + core).wait_send()

        @pl.when(step < depth // 2 - 1)
        def _():
            go_left(lax.rem(z + step, depth) * 2 + core).wait_send()

        return carry

    lax.fori_loop(0, depth, left_ring, 0)

    def left_first(root, carry):
        @pl.when(root % side != y)
        def _():
            first_a(root).wait_send()

        @pl.when(root // side != x)
        def _():
            first_b(root).wait_send()

        return carry

    lax.fori_loop(0, n_dp, left_first, 0)

    def left_second(step, carry):
        @pl.when(step != x)
        def _():
            second_a(step).wait_send()

        @pl.when(step != y)
        def _():
            second_b(step).wait_send()

        return carry

    lax.fori_loop(0, side, left_second, 0)

    def left_rot(group, carry):
        @pl.when(group != dp)
        def _():
            rot_copy(group).wait_send()

        return carry

    lax.fori_loop(0, groups, left_rot, 0)

    @pl.when(dp < groups)
    def _():
        def told(step, carry):
            pull_copy(dp, lax.rem(dp + step, n_dp)).wait_send()
            return carry

        lax.fori_loop(1, n_dp, told, 0)


def body(side, depth, grad_out, route_ids, route_weights, hidden_act, down_weight, skew_param):
    tokens, feat = grad_out.shape
    local, slots_here, hidden = hidden_act.shape
    blocks, size = skew_param.shape[1], skew_param.shape[2]
    groups = local * blocks // PER
    n_dp = side * side
    half = hidden // 2
    wide = PER * size
    act = jnp.pad(hidden_act, ((0, 0), (0, DEEP - slots_here), (0, 0)))
    vmem = pl.BlockSpec(memory_space=pltpu.VMEM)
    dma = pltpu.SemaphoreType.DMA
    hid, skg = pl.pallas_call(
        functools.partial(kernel, side, depth, groups),
        out_shape=(
            jax.ShapeDtypeStruct((local, DEEP, hidden), BF16),
            jax.ShapeDtypeStruct((groups, wide, size), F32),
        ),
        in_specs=[vmem] * 6,
        out_specs=(vmem, vmem),
        scratch_shapes=[
            pltpu.VMEM((2 * depth, tokens + 16, feat), BF16),
            pltpu.VMEM((n_dp, 2, 2 * HEAD, half), BF16),
            pltpu.VMEM((side, side - 1, 2 * HEAD, half), BF16),
            pltpu.VMEM((side, side - 1, 2 * HEAD, half), BF16),
            pltpu.VMEM((side, 2 * HEAD, half), BF16),
            pltpu.VMEM((side, 2 * HEAD, half), BF16),
            pltpu.VMEM((side - 1, 2 * HEAD, half), BF16),
            pltpu.VMEM((side - 1, 2 * HEAD, half), BF16),
            pltpu.VMEM((local, DEEP, hidden), BF16),
            pltpu.VMEM((groups, wide, wide), BF16),
            pltpu.VMEM((groups, size, wide), BF16),
            pltpu.VMEM((n_dp, size, wide), BF16),
            pltpu.VMEM((groups, size, wide), BF16),
            pltpu.VMEM((wide, wide), F32),
            pltpu.VMEM((wide, wide), BF16),
            pltpu.VMEM((5, wide, wide), BF16),
            pltpu.VMEM((6, size, wide), BF16),
            pltpu.VMEM((14, size, wide), F32),
            dma((depth,)), dma((depth,)), dma((depth,)), dma((2 * depth,)),
            dma((n_dp,)), dma((n_dp,)), dma((side, side - 1)), dma((side, side - 1)),
            dma((side,)), dma((side,)), dma((side - 1,)), dma((side - 1,)),
            dma((groups,)), dma((n_dp,)), dma((n_dp,)), dma((groups,)),
        ],
        compiler_params=pltpu.CompilerParams(
            collective_id=0, has_side_effects=True, vmem_limit_bytes=50 * 1024 * 1024
        ),
    )(
        route_ids.T, route_weights.T, grad_out, act, down_weight,
        skew_param.reshape(groups, wide, size),
    )
    return hid[:, :slots_here], skg.reshape(skew_param.shape)


def solution(mesh):
    in_specs = (
        P("expert", "dp"),
        P("expert", None),
        P("expert", None),
        P("expert", "dp", None),
        P("expert", None, "dp"),
        P("expert", None, None, None),
    )
    out_specs = (P("expert", "dp", None), P("expert", None, None, None))
    side = {4: 2, 16: 4}[mesh.shape["dp"]]
    return jax.shard_map(
        functools.partial(body, side, mesh.shape["expert"] // 2),
        mesh=mesh, in_specs=in_specs, out_specs=out_specs, check_vma=False,
    )
```

```python
import functools

import jax
import jax.numpy as jnp
from jax import lax
from jax.experimental import pallas as pl
from jax.experimental.pallas import tpu as pltpu
from jax.sharding import PartitionSpec as P

F32 = jnp.float32
BF16 = jnp.bfloat16
MESH = pl.DeviceIdType.MESH
MOST = 17
PER = 4
HEAD = 40
DEEP = 48


def dot(a, b, dims=((1,), (0,))):
    return lax.dot_general(a, b, (dims, ((), ())), preferred_element_type=F32)


def halves(value):
    high = value.astype(BF16)
    return high, (value - high.astype(F32)).astype(BF16)


def spread(slab, mask):
    return jnp.concatenate([slab] * PER, axis=0) * mask


def fold(square):
    size = square.shape[0] // PER
    total = square[:size]
    for band in range(1, PER):
        total = total + square[band * size : (band + 1) * size]
    return total


def both(slab, mask):
    high, low = halves(slab)
    return spread(high, mask), spread(low, mask)


def times(left, right):
    rows = left.shape[0]
    high, low = halves(left)
    first = dot(jnp.concatenate([high, low], axis=0), right[0])
    return first[:rows] + first[rows:] + dot(high, right[1])


def negated_skew(stack, mask):
    square = spread(stack.T, mask)
    return fold(square - square.T)


def kernel(
    side, depth, groups,
    ids_in, wts_in, grad_in, act_in, w_in, skew_in,
    hid_ref, skg_ref,
    ids_ref, wts_ref, act_ref, w_ref, skew_ref,
    gath, part, rxa, rxb, mida, midb, tra, trb, rgs, rotm, rotp, rotrx, pull, maskf, maskb, bys, lefts, values,
    s_far, s_near, s_two, s_sib, r_gath, s_in, s_a, s_b, r_a, r_b, s_ma, s_mb, r_ma, r_mb,
    s_rot, r_rot, s_pull, r_pull,
):
    n_dp = side * side
    dp = lax.axis_index("dp")
    ex = lax.axis_index("expert")
    x, y = dp // side, dp % side
    z, core = ex // 2, ex % 2
    hidden = w_ref.shape[1]
    half = hidden // 2
    size = skew_ref.shape[1] // PER
    per_expert = groups // 2
    quarter = depth // 4

    def at_z(step):
        chip = lax.rem(z + step + depth, depth)
        return chip, chip * 2 + core

    sibling = z * 2 + (1 - core)

    def copy(src, dst, send, recv, to_dp, to_ex):
        return pltpu.make_async_remote_copy(
            src_ref=src, dst_ref=dst, send_sem=send, recv_sem=recv,
            device_id=(to_dp, to_ex), device_id_type=MESH,
        )

    own = ex
    tokens = grad_in.shape[0]
    loads = [
        pltpu.make_async_copy(src, dst, s_in.at[n])
        for n, (src, dst) in enumerate((
            (ids_in, ids_ref), (wts_in, wts_ref), (grad_in, gath.at[own, pl.ds(0, tokens)]),
            (w_in, w_ref), (skew_in, skew_ref), (act_in, act_ref),
        ))
    ]
    for load in loads:
        load.start()

    barrier = pltpu.get_barrier_semaphore()
    near_steps = sorted({1, depth - 1, 2, depth - 2, quarter, depth - quarter, 2 * quarter})
    for peer in [sibling] + [at_z(step)[1] for step in near_steps]:
        pl.semaphore_signal(barrier, inc=1, device_id=(dp, peer), device_id_type=MESH)

    def greet(step, carry):
        pl.semaphore_signal(
            barrier, inc=1, device_id=(lax.rem(dp + step, n_dp), ex), device_id_type=MESH
        )
        return carry

    lax.fori_loop(1, n_dp, greet, 0)

    for load in loads[:2]:
        load.wait()
    weight = wts_ref[...]
    w1 = weight.astype(BF16).astype(F32)
    w2 = (weight - w1).astype(BF16).astype(F32)
    w3 = weight - w1 - w2
    info = jnp.concatenate(
        [
            jnp.concatenate([ids_ref[...].astype(F32), w1], axis=1),
            jnp.concatenate([w2, w3], axis=1),
        ],
        axis=0,
    )
    gath[own, tokens : tokens + 16, :] = info.astype(BF16)

    row_i = lax.broadcasted_iota(jnp.int32, (PER * size, PER * size), 0) // size
    col_i = lax.broadcasted_iota(jnp.int32, (PER * size, PER * size), 1) // size
    maskf[...] = (row_i == col_i).astype(F32)
    maskb[...] = (row_i == col_i).astype(F32).astype(BF16)

    loads[2].wait()
    pl.semaphore_wait(barrier, n_dp - 1 + 1 + len(near_steps))

    turns = (0, quarter, depth - quarter, 2 * quarter)

    def send(block, sem, to_ex):
        return copy(gath.at[block], gath.at[block], sem, r_gath.at[block], dp, to_ex)

    def go_far(n):
        return send(own, s_far.at[n], at_z(turns[n + 1])[1])

    def go_near(n, down):
        return send(at_z(turns[n])[1], s_near.at[n, down], at_z(-1 if down else 1)[1])

    def go_two(n):
        which, step = ((0, 2), (0, -2), (2, 2), (1, -2))[n]
        return send(at_z(turns[which])[1], s_two.at[n], at_z(step)[1])

    def go_across(chip):
        block = chip * 2 + core
        return send(block, s_sib.at[chip], sibling)

    for n in range(2):
        go_far(n).start()
    go_near(0, 0).start()
    go_near(0, 1).start()
    go_far(2).start()
    go_two(0).start()
    go_two(1).start()
    go_across(z).start()

    upper = (
        lax.broadcasted_iota(jnp.int32, (tokens, tokens), 0)
        < lax.broadcasted_iota(jnp.int32, (tokens, tokens), 1)
    ).astype(F32).astype(BF16)

    def rows_of(root):
        hits, heavy = [], []
        for turn in range(2):
            data = gath[root * 2 + turn, tokens : tokens + 16, :].astype(F32)
            named = data[0:8, 0:tokens]
            weights = data[0:8, tokens:] + data[8:16, 0:tokens] + data[8:16, tokens:]
            for local in range(2):
                hit = (named == (ex * 2 + local).astype(F32)).astype(F32)
                hits.append(jnp.sum(hit, axis=0, keepdims=True))
                heavy.append(jnp.sum(hit * weights, axis=0, keepdims=True))
        taken = jnp.concatenate(hits + [jnp.zeros((4, tokens), F32)], axis=0)
        rank = dot(taken.astype(BF16), upper)
        place = lax.broadcasted_iota(jnp.int32, (HEAD, tokens), 0).astype(F32)
        picks, scales = [], []
        for local in range(2):
            chosen, scale = [], None
            for turn in range(2):
                at = turn * 2 + local
                slot = jnp.where(
                    taken[at : at + 1] > 0, rank[at : at + 1] + float(turn * MOST), -1.0
                )
                equal = place == slot
                chosen.append(equal.astype(F32))
                term = jnp.sum(jnp.where(equal, heavy[at], 0.0), axis=1, keepdims=True)
                scale = term if scale is None else scale + term
            picks.append(jnp.concatenate(chosen, axis=1))
            scales.append(scale)
        pick = jnp.concatenate(picks, axis=0).astype(BF16)
        rows = jnp.concatenate(
            [gath[root * 2, 0:tokens, :], gath[root * 2 + 1, 0:tokens, :]], axis=0
        )
        routed = dot(pick, rows)
        return [routed[local * HEAD : (local + 1) * HEAD] * scales[local] for local in range(2)]

    def process(roots):
        found = [rows_of(root) for root in roots]
        sums = []
        for local in range(2):
            lhs = jnp.concatenate([f[local] for f in found], axis=0).astype(BF16)
            sums.append(dot(lhs, w_ref[local], ((1,), (1,))))
        for n, root in enumerate(roots):
            for which in range(2):
                part[root, which] = jnp.concatenate(
                    [
                        s[n * HEAD : (n + 1) * HEAD, which * half : (which + 1) * half]
                        for s in sums
                    ],
                    axis=0,
                ).astype(BF16)
            jx, jy = root // side, root % side

            @pl.when(jy != y)
            def _():
                first_a(root).start()

            @pl.when(jx != x)
            def _():
                first_b(root).start()

    def first_a(root):
        jx, jy = root // side, root % side
        off = lax.rem(jy - y + side, side)
        slot = jnp.maximum(off - 1, 0)
        return copy(part.at[root, 0], rxa.at[jx, slot], s_a.at[root], r_a.at[jx, slot], x * side + jy, ex)

    def first_b(root):
        jx, jy = root // side, root % side
        off = lax.rem(jx - x + side, side)
        slot = jnp.maximum(off - 1, 0)
        return copy(part.at[root, 1], rxb.at[jy, slot], s_b.at[root], r_b.at[jy, slot], jx * side + y, ex)

    def arrived(block):
        send(block, s_sib.at[0], sibling).wait_recv()

    def take(roots):
        for root in roots:
            go_across(root).start()
        for root in roots:
            arrived(root * 2 + 1 - core)
        process(roots)

    arrived(sibling)
    loads[3].wait()
    process([z])
    ahead, behind, far = (at_z(turns[n]) for n in (1, 2, 3))
    arrived(ahead[1])
    go_near(1, 0).start()
    go_near(1, 1).start()
    go_two(3).start()
    arrived(behind[1])
    go_near(2, 0).start()
    go_near(2, 1).start()
    go_two(2).start()
    take([ahead[0], behind[0]])
    arrived(far[1])
    go_near(3, 0).start()
    go_near(3, 1).start()
    take([far[0]])

    def beside(step, carry):
        low, high = at_z(step * quarter - 1), at_z(step * quarter + 1)
        arrived(low[1])
        arrived(high[1])
        take([low[0], high[0]])
        return carry

    def opposite(step, carry):
        low, high = at_z(step * quarter + 2), at_z((step + 2) * quarter + 2)
        arrived(low[1])
        arrived(high[1])
        take([low[0], high[0]])
        return carry

    lax.fori_loop(0, 4, beside, 0)
    lax.fori_loop(0, 2, opposite, 0)
    loads[4].wait()
    loads[5].wait()

    eye = (
        lax.broadcasted_iota(jnp.int32, (size, PER * size), 0)
        == lax.rem(lax.broadcasted_iota(jnp.int32, (size, PER * size), 1), size)
    ).astype(F32)

    def turn(group, carry):
        mask = maskb[...]
        first = negated_skew(skew_ref[group], maskf[...])
        by_first = both(first, mask)
        second = times(first, by_first)
        series = eye + first
        pair = times(jnp.concatenate([second, series], axis=0), both(second, mask))
        fourth, series = pair[:size], series + pair[size:]
        pair = times(jnp.concatenate([fourth, series], axis=0), both(fourth, mask))
        eighth, series = pair[:size], series + pair[size:]
        series = series + times(series, both(eighth, mask))
        result = series + times(series, by_first)
        rotm[group] = spread(result.astype(BF16), mask)
        return carry

    lax.fori_loop(0, groups, turn, 0)

    def prepare():
        mask = maskb[...]
        given = -negated_skew(skew_ref[jnp.minimum(dp, groups - 1)], maskf[...])

        def keep(which, slab):
            right = both(slab, mask)
            bys[which] = right[0]
            return right

        second = times(given, keep(0, given))
        one = eye + given
        pair = times(jnp.concatenate([second, one], axis=0), keep(1, second))
        fourth, two = pair[:size], one + pair[size:]
        pair = times(jnp.concatenate([fourth, two], axis=0), keep(2, fourth))
        eighth, three = pair[:size], two + pair[size:]
        keep(4, three + times(three, keep(3, eighth)))
        for which, slab in enumerate((given, second, one, fourth, two, three)):
            lefts[which] = slab.astype(BF16)

    prepare()

    def gather_a(jx, carry):
        root = jx * side + y
        total = part[root, 0].astype(F32)
        for slot in range(side - 1):
            copy(part.at[root, 0], rxa.at[jx, slot], s_a.at[root], r_a.at[jx, slot], dp, ex).wait_recv()
            total = total + rxa[jx, slot].astype(F32)
        mida[jx] = total.astype(BF16)

        @pl.when(jx != x)
        def _():
            second_a(jx).start()

        return carry

    def second_a(jx):
        slot = jnp.maximum(lax.rem(jx - x + side, side) - 1, 0)
        return copy(mida.at[jx], tra.at[slot], s_ma.at[jx], r_ma.at[slot], jx * side + y, ex)

    def gather_b(jy, carry):
        root = x * side + jy
        total = part[root, 1].astype(F32)
        for slot in range(side - 1):
            copy(part.at[root, 1], rxb.at[jy, slot], s_b.at[root], r_b.at[jy, slot], dp, ex).wait_recv()
            total = total + rxb[jy, slot].astype(F32)
        midb[jy] = total.astype(BF16)

        @pl.when(jy != y)
        def _():
            second_b(jy).start()

        return carry

    def second_b(jy):
        slot = jnp.maximum(lax.rem(jy - y + side, side) - 1, 0)
        return copy(midb.at[jy], trb.at[slot], s_mb.at[jy], r_mb.at[slot], x * side + jy, ex)

    def gather_both(step, carry):
        gather_a(step, 0)
        gather_b(step, 0)
        return carry

    lax.fori_loop(0, side, gather_both, 0)

    for which, (mid, at, tr, s_m, r_m) in enumerate(((mida, x, tra, s_ma, r_ma), (midb, y, trb, s_mb, r_mb))):
        total = mid[at].astype(F32)
        for slot in range(side - 1):
            copy(mid.at[0], tr.at[slot], s_m.at[0], r_m.at[slot], dp, ex).wait_recv()
            total = total + tr[slot].astype(F32)
        for local in range(2):
            rgs[local, :, which * half : (which + 1) * half] = jnp.concatenate(
                [total[local * HEAD : (local + 1) * HEAD], jnp.zeros((DEEP - HEAD, half), F32)], axis=0
            ).astype(BF16)

    def lanes_of(group):
        return pl.ds(pl.multiple_of((group % per_expert) * PER * size, PER * size), PER * size)

    def rot_copy(group):
        return copy(rotp.at[group], rotrx.at[dp], s_rot.at[group], r_rot.at[dp], group, ex)

    def grads(group, carry):
        local, lanes = group // per_expert, lanes_of(group)
        square = dot(act_ref[local, :, lanes], rgs[local, :, lanes], ((0,), (0,)))
        rotp[group] = fold(square * maskf[...]).astype(BF16)

        @pl.when(group != dp)
        def _():
            rot_copy(group).start()

        return carry

    lax.fori_loop(0, groups, grads, 0)

    def hide(group, carry):
        local, lanes = group // per_expert, lanes_of(group)
        hid_ref[local, :, lanes] = dot(rgs[local, :, lanes], rotm[group], ((1,), (1,))).astype(BF16)
        return carry

    lax.fori_loop(0, groups, hide, 0)

    def pull_copy(owner, peer):
        return copy(pull.at[owner], pull.at[owner], s_pull.at[peer], r_pull.at[owner], peer, ex)

    @pl.when(dp < groups)
    def _():
        mask = maskb[...]

        def add(step, total):
            source = lax.rem(dp + step, n_dp)
            copy(rotp.at[0], rotrx.at[source], s_rot.at[0], r_rot.at[source], dp, ex).wait_recv()
            return total + rotrx[source].astype(F32)

        change = lax.fori_loop(1, n_dp, add, rotp[dp].astype(F32))
        change_b = change.astype(BF16)

        none = dp // n_dp

        def put(at, left, right):
            rows = left.shape[0] // size
            values[at : at + rows] = dot(left, right).reshape(rows, size, PER * size)
            return [values[at + row + none] for row in range(rows)]

        def rows_at(first, count):
            return lefts[first : first + count].reshape(count * size, PER * size)

        (front,) = put(0, rows_at(0, 1), spread(change_b, mask))
        (back,) = put(1, change_b, bys[0])
        change2 = (front + back).astype(BF16)
        front, lower = put(2, rows_at(1, 2), spread(change2, mask))
        (back,) = put(4, change2, bys[1])
        change4 = (front + back).astype(BF16)
        (back,) = put(5, change_b, bys[1])
        two_change = change + back + lower
        front, lower = put(6, rows_at(3, 2), spread(change4, mask))
        (back,) = put(8, change4, bys[2])
        change8 = (front + back).astype(BF16)
        (back,) = put(9, two_change.astype(BF16), bys[2])
        three_change = two_change + back + lower
        (lower,) = put(10, rows_at(5, 1), spread(change8, mask))
        (back,) = put(11, three_change.astype(BF16), bys[3])
        four_change = three_change + back + lower
        (front,) = put(12, rows_at(0, 1), spread(four_change.astype(BF16), mask))
        (back,) = put(13, change_b, bys[4])
        result = front + four_change + back
        square = spread(result, maskf[...])
        pull[dp] = fold(square.T - square).astype(BF16)

        def tell(step, carry):
            pull_copy(dp, lax.rem(dp + step, n_dp)).start()
            return carry

        lax.fori_loop(1, n_dp, tell, 0)

    def write(group, carry):
        @pl.when(group != dp)
        def _():
            pull_copy(group, dp).wait_recv()

        skg_ref[group] = -(pull[group].astype(F32).T)
        return carry

    lax.fori_loop(0, groups, write, 0)

    for n in range(3):
        go_far(n).wait_send()
    for n in range(4):
        go_near(n, 0).wait_send()
        go_near(n, 1).wait_send()
        go_two(n).wait_send()

    def left_across(chip, carry):
        go_across(chip).wait_send()
        return carry

    lax.fori_loop(0, depth, left_across, 0)

    def left_first(root, carry):
        @pl.when(root % side != y)
        def _():
            first_a(root).wait_send()

        @pl.when(root // side != x)
        def _():
            first_b(root).wait_send()

        return carry

    lax.fori_loop(0, n_dp, left_first, 0)

    def left_second(step, carry):
        @pl.when(step != x)
        def _():
            second_a(step).wait_send()

        @pl.when(step != y)
        def _():
            second_b(step).wait_send()

        return carry

    lax.fori_loop(0, side, left_second, 0)

    def left_rot(group, carry):
        @pl.when(group != dp)
        def _():
            rot_copy(group).wait_send()

        return carry

    lax.fori_loop(0, groups, left_rot, 0)

    @pl.when(dp < groups)
    def _():
        def told(step, carry):
            pull_copy(dp, lax.rem(dp + step, n_dp)).wait_send()
            return carry

        lax.fori_loop(1, n_dp, told, 0)


def body(side, depth, grad_out, route_ids, route_weights, hidden_act, down_weight, skew_param):
    tokens, feat = grad_out.shape
    local, slots_here, hidden = hidden_act.shape
    blocks, size = skew_param.shape[1], skew_param.shape[2]
    groups = local * blocks // PER
    n_dp = side * side
    half = hidden // 2
    wide = PER * size
    act = jnp.pad(hidden_act, ((0, 0), (0, DEEP - slots_here), (0, 0)))
    vmem = pl.BlockSpec(memory_space=pltpu.VMEM)
    dma = pltpu.SemaphoreType.DMA
    hid, skg = pl.pallas_call(
        functools.partial(kernel, side, depth, groups),
        out_shape=(
            jax.ShapeDtypeStruct((local, DEEP, hidden), BF16),
            jax.ShapeDtypeStruct((groups, wide, size), F32),
        ),
        in_specs=[pl.BlockSpec(memory_space=pltpu.HBM)] * 6,
        out_specs=(vmem, vmem),
        scratch_shapes=[
            pltpu.VMEM((8, tokens), jnp.int32),
            pltpu.VMEM((8, tokens), F32),
            pltpu.VMEM((local, DEEP, hidden), BF16),
            pltpu.VMEM((local, hidden, feat), BF16),
            pltpu.VMEM((groups, wide, size), F32),
            pltpu.VMEM((2 * depth, tokens + 16, feat), BF16),
            pltpu.VMEM((n_dp, 2, 2 * HEAD, half), BF16),
            pltpu.VMEM((side, side - 1, 2 * HEAD, half), BF16),
            pltpu.VMEM((side, side - 1, 2 * HEAD, half), BF16),
            pltpu.VMEM((side, 2 * HEAD, half), BF16),
            pltpu.VMEM((side, 2 * HEAD, half), BF16),
            pltpu.VMEM((side - 1, 2 * HEAD, half), BF16),
            pltpu.VMEM((side - 1, 2 * HEAD, half), BF16),
            pltpu.VMEM((local, DEEP, hidden), BF16),
            pltpu.VMEM((groups, wide, wide), BF16),
            pltpu.VMEM((groups, size, wide), BF16),
            pltpu.VMEM((n_dp, size, wide), BF16),
            pltpu.VMEM((groups, size, wide), BF16),
            pltpu.VMEM((wide, wide), F32),
            pltpu.VMEM((wide, wide), BF16),
            pltpu.VMEM((5, wide, wide), BF16),
            pltpu.VMEM((6, size, wide), BF16),
            pltpu.VMEM((14, size, wide), F32),
            dma((3,)), dma((4, 2)), dma((4,)), dma((depth,)), dma((2 * depth,)), dma((6,)),
            dma((n_dp,)), dma((n_dp,)), dma((side, side - 1)), dma((side, side - 1)),
            dma((side,)), dma((side,)), dma((side - 1,)), dma((side - 1,)),
            dma((groups,)), dma((n_dp,)), dma((n_dp,)), dma((groups,)),
        ],
        compiler_params=pltpu.CompilerParams(
            collective_id=0, has_side_effects=True, vmem_limit_bytes=63 * 1024 * 1024
        ),
    )(
        route_ids.T, route_weights.T, grad_out, act, down_weight,
        skew_param.reshape(groups, wide, size),
    )
    return hid[:, :slots_here], skg.reshape(skew_param.shape)


def solution(mesh):
    in_specs = (
        P("expert", "dp"),
        P("expert", None),
        P("expert", None),
        P("expert", "dp", None),
        P("expert", None, "dp"),
        P("expert", None, None, None),
    )
    out_specs = (P("expert", "dp", None), P("expert", None, None, None))
    side = {4: 2, 16: 4}[mesh.shape["dp"]]
    return jax.shard_map(
        functools.partial(body, side, mesh.shape["expert"] // 2),
        mesh=mesh, in_specs=in_specs, out_specs=out_specs, check_vma=False,
    )
```

```python
import functools

import jax
import jax.numpy as jnp
from jax import lax
from jax.experimental import pallas as pl
from jax.experimental.pallas import tpu as pltpu
from jax.sharding import PartitionSpec as P

F32 = jnp.float32
BF16 = jnp.bfloat16
MESH = pl.DeviceIdType.MESH
MOST = 17
PER = 4
HEAD = 40
DEEP = 48


def dot(a, b, dims=((1,), (0,))):
    return lax.dot_general(a, b, (dims, ((), ())), preferred_element_type=F32)


def halves(value):
    high = value.astype(BF16)
    return high, (value - high.astype(F32)).astype(BF16)


def spread(slab, mask):
    return jnp.concatenate([slab] * PER, axis=0) * mask


def fold(square):
    size = square.shape[0] // PER
    total = square[:size]
    for band in range(1, PER):
        total = total + square[band * size : (band + 1) * size]
    return total


def both(slab, mask):
    high, low = halves(slab)
    return spread(high, mask), spread(low, mask)


def times(left, right):
    rows = left.shape[0]
    high, low = halves(left)
    first = dot(jnp.concatenate([high, low], axis=0), right[0])
    return first[:rows] + first[rows:] + dot(high, right[1])


def negated_skew(stack, mask):
    square = spread(stack.T, mask)
    return fold(square - square.T)


def kernel(
    side, depth, groups,
    ids_ref, wts_ref, grad_ref, act_ref, w_ref, skew_ref,
    hid_ref, skg_ref,
    gath, part, rxa, rxb, mida, midb, tra, trb, rgs, rotm, rotp, rotrx, pull, maskf, maskb, bys, lefts, values,
    s_right, s_left, s_far, s_sib, r_gath, s_a, s_b, r_a, r_b, s_ma, s_mb, r_ma, r_mb,
    s_rot, r_rot, s_pull, r_pull,
):
    n_dp = side * side
    dp = lax.axis_index("dp")
    ex = lax.axis_index("expert")
    x, y = dp // side, dp % side
    z, core = ex // 2, ex % 2
    hidden = w_ref.shape[1]
    half = hidden // 2
    size = skew_ref.shape[1] // PER
    per_expert = groups // 2
    jump = 5

    def at_z(step):
        chip = lax.rem(z + step + depth, depth)
        return chip, chip * 2 + core

    right, left = at_z(1)[1], at_z(-1)[1]
    beyond, before = at_z(jump)[1], at_z(-jump)[1]
    sibling = z * 2 + (1 - core)

    def copy(src, dst, send, recv, to_dp, to_ex):
        return pltpu.make_async_remote_copy(
            src_ref=src, dst_ref=dst, send_sem=send, recv_sem=recv,
            device_id=(to_dp, to_ex), device_id_type=MESH,
        )

    barrier = pltpu.get_barrier_semaphore()
    for peer in (right, left, beyond, before, sibling):
        pl.semaphore_signal(barrier, inc=1, device_id=(dp, peer), device_id_type=MESH)

    def greet(step, carry):
        pl.semaphore_signal(
            barrier, inc=1, device_id=(lax.rem(dp + step, n_dp), ex), device_id_type=MESH
        )
        return carry

    lax.fori_loop(1, n_dp, greet, 0)

    tokens = grad_ref.shape[0]
    own = ex
    gath[own, 0:tokens, :] = grad_ref[...]
    weight = wts_ref[...]
    w1 = weight.astype(BF16).astype(F32)
    w2 = (weight - w1).astype(BF16).astype(F32)
    w3 = weight - w1 - w2
    info = jnp.concatenate(
        [
            jnp.concatenate([ids_ref[...].astype(F32), w1], axis=1),
            jnp.concatenate([w2, w3], axis=1),
        ],
        axis=0,
    )
    gath[own, tokens : tokens + 16, :] = info.astype(BF16)

    row_i = lax.broadcasted_iota(jnp.int32, (PER * size, PER * size), 0) // size
    col_i = lax.broadcasted_iota(jnp.int32, (PER * size, PER * size), 1) // size
    maskf[...] = (row_i == col_i).astype(F32)
    maskb[...] = (row_i == col_i).astype(F32).astype(BF16)

    pl.semaphore_wait(barrier, n_dp - 1 + 5)

    def go_right(block):
        return copy(gath.at[block], gath.at[block], s_right.at[block // 2], r_gath.at[block], dp, right)

    def go_left(block):
        return copy(gath.at[block], gath.at[block], s_left.at[block // 2], r_gath.at[block], dp, left)

    def go_across(block):
        return copy(gath.at[block], gath.at[block], s_sib.at[block // 2], r_gath.at[block], dp, sibling)

    def go_far(n):
        return copy(
            gath.at[own], gath.at[own], s_far.at[n], r_gath.at[own], dp, (beyond, before)[n]
        )

    go_far(0).start()
    go_far(1).start()
    go_right(own).start()
    go_left(own).start()
    go_across(own).start()

    upper = (
        lax.broadcasted_iota(jnp.int32, (tokens, tokens), 0)
        < lax.broadcasted_iota(jnp.int32, (tokens, tokens), 1)
    ).astype(F32).astype(BF16)

    def rows_of(root):
        hits, heavy = [], []
        for turn in range(2):
            data = gath[root * 2 + turn, tokens : tokens + 16, :].astype(F32)
            named = data[0:8, 0:tokens]
            weights = data[0:8, tokens:] + data[8:16, 0:tokens] + data[8:16, tokens:]
            for local in range(2):
                hit = (named == (ex * 2 + local).astype(F32)).astype(F32)
                hits.append(jnp.sum(hit, axis=0, keepdims=True))
                heavy.append(jnp.sum(hit * weights, axis=0, keepdims=True))
        taken = jnp.concatenate(hits + [jnp.zeros((4, tokens), F32)], axis=0)
        rank = dot(taken.astype(BF16), upper)
        place = lax.broadcasted_iota(jnp.int32, (HEAD, tokens), 0).astype(F32)
        picks, scales = [], []
        for local in range(2):
            chosen, scale = [], None
            for turn in range(2):
                at = turn * 2 + local
                slot = jnp.where(
                    taken[at : at + 1] > 0, rank[at : at + 1] + float(turn * MOST), -1.0
                )
                equal = place == slot
                chosen.append(equal.astype(F32))
                term = jnp.sum(jnp.where(equal, heavy[at], 0.0), axis=1, keepdims=True)
                scale = term if scale is None else scale + term
            picks.append(jnp.concatenate(chosen, axis=1))
            scales.append(scale)
        pick = jnp.concatenate(picks, axis=0).astype(BF16)
        rows = jnp.concatenate(
            [gath[root * 2, 0:tokens, :], gath[root * 2 + 1, 0:tokens, :]], axis=0
        )
        routed = dot(pick, rows)
        return [routed[local * HEAD : (local + 1) * HEAD] * scales[local] for local in range(2)]

    def process(roots):
        found = [rows_of(root) for root in roots]
        sums = []
        for local in range(2):
            lhs = jnp.concatenate([f[local] for f in found], axis=0).astype(BF16)
            sums.append(dot(lhs, w_ref[local], ((1,), (1,))))
        for n, root in enumerate(roots):
            for which in range(2):
                part[root, which] = jnp.concatenate(
                    [
                        s[n * HEAD : (n + 1) * HEAD, which * half : (which + 1) * half]
                        for s in sums
                    ],
                    axis=0,
                ).astype(BF16)
            jx, jy = root // side, root % side

            @pl.when(jy != y)
            def _():
                first_a(root).start()

            @pl.when(jx != x)
            def _():
                first_b(root).start()

    def first_a(root):
        jx, jy = root // side, root % side
        off = lax.rem(jy - y + side, side)
        slot = jnp.maximum(off - 1, 0)
        return copy(part.at[root, 0], rxa.at[jx, slot], s_a.at[root], r_a.at[jx, slot], x * side + jy, ex)

    def first_b(root):
        jx, jy = root // side, root % side
        off = lax.rem(jx - x + side, side)
        slot = jnp.maximum(off - 1, 0)
        return copy(part.at[root, 1], rxb.at[jy, slot], s_b.at[root], r_b.at[jy, slot], jx * side + y, ex)

    def arrived(block):
        go_right(block).wait_recv()

    def get(step, on_right=False, on_left=False):
        block = at_z(step)[1]
        arrived(block)
        if on_right:
            go_right(block).start()
        if on_left:
            go_left(block).start()
        go_across(block).start()

    arrived(sibling)
    process([z])
    steps = (
        (1, ((1, False, True), (-1, True, False))),
        (5, ((5, True, True), (-5, True, True))),
        (2, ((2, False, False), (-2, False, False))),
        (4, ((4, True, False), (-6, True, False), (6, False, True), (-4, False, True))),
        (6, ((-7, True, False), (7, False, False))),
        (3, ((3, False, False), (-3, False, False))),
        (7, ((8, False, False),)),
    )

    def ring(turn, carry):
        step = 0
        for n, (away, blocks) in enumerate(steps):
            step = step + jnp.where(turn == n, away, 0)

            @pl.when(turn == n)
            def _():
                for block in blocks:
                    get(*block)

        low, high = at_z(-step)[0], at_z(step)[0]
        arrived(low * 2 + 1 - core)
        arrived(high * 2 + 1 - core)
        process([low, high])
        return carry

    lax.fori_loop(0, len(steps), ring, 0)
    far = at_z(8)[0]
    arrived(far * 2 + 1 - core)
    process([far])

    eye = (
        lax.broadcasted_iota(jnp.int32, (size, PER * size), 0)
        == lax.rem(lax.broadcasted_iota(jnp.int32, (size, PER * size), 1), size)
    ).astype(F32)

    def turn(group, carry):
        mask = maskb[...]
        first = negated_skew(skew_ref[group], maskf[...])
        by_first = both(first, mask)
        second = times(first, by_first)
        series = eye + first
        pair = times(jnp.concatenate([second, series], axis=0), both(second, mask))
        fourth, series = pair[:size], series + pair[size:]
        pair = times(jnp.concatenate([fourth, series], axis=0), both(fourth, mask))
        eighth, series = pair[:size], series + pair[size:]
        series = series + times(series, both(eighth, mask))
        result = series + times(series, by_first)
        rotm[group] = spread(result.astype(BF16), mask)
        return carry

    lax.fori_loop(0, groups, turn, 0)

    def prepare():
        mask = maskb[...]
        given = -negated_skew(skew_ref[jnp.minimum(dp, groups - 1)], maskf[...])

        def keep(which, slab):
            right = both(slab, mask)
            bys[which] = right[0]
            return right

        second = times(given, keep(0, given))
        one = eye + given
        pair = times(jnp.concatenate([second, one], axis=0), keep(1, second))
        fourth, two = pair[:size], one + pair[size:]
        pair = times(jnp.concatenate([fourth, two], axis=0), keep(2, fourth))
        eighth, three = pair[:size], two + pair[size:]
        keep(4, three + times(three, keep(3, eighth)))
        for which, slab in enumerate((given, second, one, fourth, two, three)):
            lefts[which] = slab.astype(BF16)

    prepare()

    def gather_a(jx, carry):
        root = jx * side + y
        total = part[root, 0].astype(F32)
        for slot in range(side - 1):
            copy(part.at[root, 0], rxa.at[jx, slot], s_a.at[root], r_a.at[jx, slot], dp, ex).wait_recv()
            total = total + rxa[jx, slot].astype(F32)
        mida[jx] = total.astype(BF16)

        @pl.when(jx != x)
        def _():
            second_a(jx).start()

        return carry

    def second_a(jx):
        slot = jnp.maximum(lax.rem(jx - x + side, side) - 1, 0)
        return copy(mida.at[jx], tra.at[slot], s_ma.at[jx], r_ma.at[slot], jx * side + y, ex)

    def gather_b(jy, carry):
        root = x * side + jy
        total = part[root, 1].astype(F32)
        for slot in range(side - 1):
            copy(part.at[root, 1], rxb.at[jy, slot], s_b.at[root], r_b.at[jy, slot], dp, ex).wait_recv()
            total = total + rxb[jy, slot].astype(F32)
        midb[jy] = total.astype(BF16)

        @pl.when(jy != y)
        def _():
            second_b(jy).start()

        return carry

    def second_b(jy):
        slot = jnp.maximum(lax.rem(jy - y + side, side) - 1, 0)
        return copy(midb.at[jy], trb.at[slot], s_mb.at[jy], r_mb.at[slot], x * side + jy, ex)

    def gather_both(step, carry):
        gather_a(lax.rem(z // side + step + step // 2 - 2 * (step // 3), side), 0)
        gather_b(lax.rem(y + 1 + step, side), 0)
        return carry

    lax.fori_loop(0, side, gather_both, 0)

    for which, (mid, at, tr, s_m, r_m) in enumerate(((mida, x, tra, s_ma, r_ma), (midb, y, trb, s_mb, r_mb))):
        total = mid[at].astype(F32)
        for slot in range(side - 1):
            copy(mid.at[0], tr.at[slot], s_m.at[0], r_m.at[slot], dp, ex).wait_recv()
            total = total + tr[slot].astype(F32)
        for local in range(2):
            rgs[local, :, which * half : (which + 1) * half] = jnp.concatenate(
                [total[local * HEAD : (local + 1) * HEAD], jnp.zeros((DEEP - HEAD, half), F32)], axis=0
            ).astype(BF16)

    def lanes_of(group):
        return pl.ds(pl.multiple_of((group % per_expert) * PER * size, PER * size), PER * size)

    def rot_copy(group):
        return copy(rotp.at[group], rotrx.at[dp], s_rot.at[group], r_rot.at[dp], group, ex)

    def grads(step, carry):
        group = lax.rem(dp + 1 + step, groups)
        local, lanes = group // per_expert, lanes_of(group)
        square = dot(act_ref[local, :, lanes], rgs[local, :, lanes], ((0,), (0,)))
        rotp[group] = fold(square * maskf[...]).astype(BF16)

        @pl.when(group != dp)
        def _():
            rot_copy(group).start()

        return carry

    lax.fori_loop(0, groups, grads, 0)

    def hide(group, carry):
        local, lanes = group // per_expert, lanes_of(group)
        hid_ref[local, :, lanes] = dot(rgs[local, :, lanes], rotm[group], ((1,), (1,))).astype(BF16)
        return carry

    lax.fori_loop(0, groups, hide, 0)

    def pull_copy(owner, peer):
        return copy(pull.at[owner], pull.at[owner], s_pull.at[peer], r_pull.at[owner], peer, ex)

    @pl.when(dp < groups)
    def _():
        mask = maskb[...]

        def add(step, total):
            source = lax.rem(dp + step, n_dp)
            copy(rotp.at[0], rotrx.at[source], s_rot.at[0], r_rot.at[source], dp, ex).wait_recv()
            return total + rotrx[source].astype(F32)

        change = lax.fori_loop(1, n_dp, add, rotp[dp].astype(F32))
        change_b = change.astype(BF16)

        none = dp // n_dp

        def put(at, left, right):
            rows = left.shape[0] // size
            values[at : at + rows] = dot(left, right).reshape(rows, size, PER * size)
            return [values[at + row + none] for row in range(rows)]

        def rows_at(first, count):
            return lefts[first : first + count].reshape(count * size, PER * size)

        (front,) = put(0, rows_at(0, 1), spread(change_b, mask))
        (back,) = put(1, change_b, bys[0])
        change2 = (front + back).astype(BF16)
        front, lower = put(2, rows_at(1, 2), spread(change2, mask))
        (back,) = put(4, change2, bys[1])
        change4 = (front + back).astype(BF16)
        (back,) = put(5, change_b, bys[1])
        two_change = change + back + lower
        front, lower = put(6, rows_at(3, 2), spread(change4, mask))
        (back,) = put(8, change4, bys[2])
        change8 = (front + back).astype(BF16)
        (back,) = put(9, two_change.astype(BF16), bys[2])
        three_change = two_change + back + lower
        (lower,) = put(10, rows_at(5, 1), spread(change8, mask))
        (back,) = put(11, three_change.astype(BF16), bys[3])
        four_change = three_change + back + lower
        (front,) = put(12, rows_at(0, 1), spread(four_change.astype(BF16), mask))
        (back,) = put(13, change_b, bys[4])
        result = front + four_change + back
        square = spread(result, maskf[...])
        pull[dp] = fold(square.T - square).astype(BF16)

        def tell(step, carry):
            pull_copy(dp, lax.rem(dp + step, n_dp)).start()
            return carry

        lax.fori_loop(1, n_dp, tell, 0)

    def write(step, carry):
        group = lax.rem(dp + groups - step, groups)

        @pl.when(group != dp)
        def _():
            pull_copy(group, dp).wait_recv()

        skg_ref[group] = -(pull[group].astype(F32).T)
        return carry

    lax.fori_loop(0, groups, write, 0)

    go_far(0).wait_send()
    go_far(1).wait_send()
    for step in (0, 5, -5, -1, 4, -6, -7):
        go_right(at_z(step)[1]).wait_send()
    for step in (0, 5, -5, 1, 6, -4):
        go_left(at_z(step)[1]).wait_send()

    def left_across(chip, carry):
        go_across(chip * 2 + core).wait_send()
        return carry

    lax.fori_loop(0, depth, left_across, 0)

    def left_first(root, carry):
        @pl.when(root % side != y)
        def _():
            first_a(root).wait_send()

        @pl.when(root // side != x)
        def _():
            first_b(root).wait_send()

        return carry

    lax.fori_loop(0, n_dp, left_first, 0)

    def left_second(step, carry):
        @pl.when(step != x)
        def _():
            second_a(step).wait_send()

        @pl.when(step != y)
        def _():
            second_b(step).wait_send()

        return carry

    lax.fori_loop(0, side, left_second, 0)

    def left_rot(group, carry):
        @pl.when(group != dp)
        def _():
            rot_copy(group).wait_send()

        return carry

    lax.fori_loop(0, groups, left_rot, 0)

    @pl.when(dp < groups)
    def _():
        def told(step, carry):
            pull_copy(dp, lax.rem(dp + step, n_dp)).wait_send()
            return carry

        lax.fori_loop(1, n_dp, told, 0)


def body(side, depth, grad_out, route_ids, route_weights, hidden_act, down_weight, skew_param):
    tokens, feat = grad_out.shape
    local, slots_here, hidden = hidden_act.shape
    blocks, size = skew_param.shape[1], skew_param.shape[2]
    groups = local * blocks // PER
    n_dp = side * side
    half = hidden // 2
    wide = PER * size
    act = jnp.pad(hidden_act, ((0, 0), (0, DEEP - slots_here), (0, 0)))
    vmem = pl.BlockSpec(memory_space=pltpu.VMEM)
    dma = pltpu.SemaphoreType.DMA
    hid, skg = pl.pallas_call(
        functools.partial(kernel, side, depth, groups),
        out_shape=(
            jax.ShapeDtypeStruct((local, DEEP, hidden), BF16),
            jax.ShapeDtypeStruct((groups, wide, size), F32),
        ),
        in_specs=[vmem] * 6,
        out_specs=(vmem, vmem),
        scratch_shapes=[
            pltpu.VMEM((2 * depth, tokens + 16, feat), BF16),
            pltpu.VMEM((n_dp, 2, 2 * HEAD, half), BF16),
            pltpu.VMEM((side, side - 1, 2 * HEAD, half), BF16),
            pltpu.VMEM((side, side - 1, 2 * HEAD, half), BF16),
            pltpu.VMEM((side, 2 * HEAD, half), BF16),
            pltpu.VMEM((side, 2 * HEAD, half), BF16),
            pltpu.VMEM((side - 1, 2 * HEAD, half), BF16),
            pltpu.VMEM((side - 1, 2 * HEAD, half), BF16),
            pltpu.VMEM((local, DEEP, hidden), BF16),
            pltpu.VMEM((groups, wide, wide), BF16),
            pltpu.VMEM((groups, size, wide), BF16),
            pltpu.VMEM((n_dp, size, wide), BF16),
            pltpu.VMEM((groups, size, wide), BF16),
            pltpu.VMEM((wide, wide), F32),
            pltpu.VMEM((wide, wide), BF16),
            pltpu.VMEM((5, wide, wide), BF16),
            pltpu.VMEM((6, size, wide), BF16),
            pltpu.VMEM((14, size, wide), F32),
            dma((depth,)), dma((depth,)), dma((2,)), dma((depth,)), dma((2 * depth,)),
            dma((n_dp,)), dma((n_dp,)), dma((side, side - 1)), dma((side, side - 1)),
            dma((side,)), dma((side,)), dma((side - 1,)), dma((side - 1,)),
            dma((groups,)), dma((n_dp,)), dma((n_dp,)), dma((groups,)),
        ],
        compiler_params=pltpu.CompilerParams(
            collective_id=0, has_side_effects=True, vmem_limit_bytes=50 * 1024 * 1024
        ),
    )(
        route_ids.T, route_weights.T, grad_out, act, down_weight,
        skew_param.reshape(groups, wide, size),
    )
    return hid[:, :slots_here], skg.reshape(skew_param.shape)


def solution(mesh):
    in_specs = (
        P("expert", "dp"),
        P("expert", None),
        P("expert", None),
        P("expert", "dp", None),
        P("expert", None, "dp"),
        P("expert", None, None, None),
    )
    out_specs = (P("expert", "dp", None), P("expert", None, None, None))
    side = {4: 2, 16: 4}[mesh.shape["dp"]]
    return jax.shard_map(
        functools.partial(body, side, mesh.shape["expert"] // 2),
        mesh=mesh, in_specs=in_specs, out_specs=out_specs, check_vma=False,
    )
```

```python
import functools

import jax
import jax.numpy as jnp
from jax import lax
from jax.experimental import pallas as pl
from jax.experimental.pallas import tpu as pltpu
from jax.sharding import PartitionSpec as P

F32 = jnp.float32
BF16 = jnp.bfloat16
MESH = pl.DeviceIdType.MESH
MOST = 17
PER = 4
HEAD = 40
DEEP = 48


def dot(a, b, dims=((1,), (0,))):
    return lax.dot_general(a, b, (dims, ((), ())), preferred_element_type=F32)


def halves(value):
    high = value.astype(BF16)
    return high, (value - high.astype(F32)).astype(BF16)


def spread(slab, mask):
    return jnp.concatenate([slab] * PER, axis=0) * mask


def fold(square):
    size = square.shape[0] // PER
    total = square[:size]
    for band in range(1, PER):
        total = total + square[band * size : (band + 1) * size]
    return total


def both(slab, mask):
    high, low = halves(slab)
    return spread(high, mask), spread(low, mask)


def times(left, right):
    rows = left.shape[0]
    high, low = halves(left)
    first = dot(jnp.concatenate([high, low], axis=0), right[0])
    return first[:rows] + first[rows:] + dot(high, right[1])


def negated_skew(stack, mask):
    square = spread(stack.T, mask)
    return fold(square - square.T)


def kernel(
    side, depth, groups,
    ids_ref, wts_ref, grad_ref, act_ref, w_ref, skew_ref,
    hid_ref, skg_ref,
    gath, part, rxa, rxb, mida, midb, tra, trb, rgs, rotm, rotp, rotrx, pull, maskf, maskb, bys, lefts, values,
    s_right, s_left, s_far, s_sib, r_gath, s_a, s_b, r_a, r_b, s_ma, s_mb, r_ma, r_mb,
    s_rot, r_rot, s_pull, r_pull,
):
    n_dp = side * side
    dp = lax.axis_index("dp")
    ex = lax.axis_index("expert")
    x, y = dp // side, dp % side
    z, core = ex // 2, ex % 2
    hidden = w_ref.shape[1]
    half = hidden // 2
    size = skew_ref.shape[1] // PER
    per_expert = groups // 2
    jump = 5

    def at_z(step):
        chip = lax.rem(z + step + depth, depth)
        return chip, chip * 2 + core

    right, left = at_z(1)[1], at_z(-1)[1]
    beyond, before = at_z(jump)[1], at_z(-jump)[1]
    sibling = z * 2 + (1 - core)

    def copy(src, dst, send, recv, to_dp, to_ex):
        return pltpu.make_async_remote_copy(
            src_ref=src, dst_ref=dst, send_sem=send, recv_sem=recv,
            device_id=(to_dp, to_ex), device_id_type=MESH,
        )

    barrier = pltpu.get_barrier_semaphore()
    for peer in (right, left, beyond, before, sibling):
        pl.semaphore_signal(barrier, inc=1, device_id=(dp, peer), device_id_type=MESH)

    def greet(step, carry):
        pl.semaphore_signal(
            barrier, inc=1, device_id=(lax.rem(dp + step, n_dp), ex), device_id_type=MESH
        )
        return carry

    lax.fori_loop(1, n_dp, greet, 0)

    tokens = grad_ref.shape[0]
    own = ex
    gath[own, 0:tokens, :] = grad_ref[...]
    weight = wts_ref[...]
    w1 = weight.astype(BF16).astype(F32)
    w2 = (weight - w1).astype(BF16).astype(F32)
    w3 = weight - w1 - w2
    info = jnp.concatenate(
        [
            jnp.concatenate([ids_ref[...].astype(F32), w1], axis=1),
            jnp.concatenate([w2, w3], axis=1),
        ],
        axis=0,
    )
    gath[own, tokens : tokens + 16, :] = info.astype(BF16)

    row_i = lax.broadcasted_iota(jnp.int32, (PER * size, PER * size), 0) // size
    col_i = lax.broadcasted_iota(jnp.int32, (PER * size, PER * size), 1) // size
    maskf[...] = (row_i == col_i).astype(F32)
    maskb[...] = (row_i == col_i).astype(F32).astype(BF16)

    pl.semaphore_wait(barrier, n_dp - 1 + 5)

    def go_right(block):
        return copy(gath.at[block], gath.at[block], s_right.at[block // 2], r_gath.at[block], dp, right)

    def go_left(block):
        return copy(gath.at[block], gath.at[block], s_left.at[block // 2], r_gath.at[block], dp, left)

    def go_across(block):
        return copy(gath.at[block], gath.at[block], s_sib.at[block // 2], r_gath.at[block], dp, sibling)

    def go_far(n):
        return copy(
            gath.at[own], gath.at[own], s_far.at[n], r_gath.at[own], dp, (beyond, before)[n]
        )

    go_far(0).start()
    go_far(1).start()
    go_right(own).start()
    go_left(own).start()
    go_across(own).start()

    upper = (
        lax.broadcasted_iota(jnp.int32, (tokens, tokens), 0)
        < lax.broadcasted_iota(jnp.int32, (tokens, tokens), 1)
    ).astype(F32).astype(BF16)

    def rows_of(root):
        hits, heavy = [], []
        for turn in range(2):
            data = gath[root * 2 + turn, tokens : tokens + 16, :].astype(F32)
            named = data[0:8, 0:tokens]
            weights = data[0:8, tokens:] + data[8:16, 0:tokens] + data[8:16, tokens:]
            for local in range(2):
                hit = (named == (ex * 2 + local).astype(F32)).astype(F32)
                hits.append(jnp.sum(hit, axis=0, keepdims=True))
                heavy.append(jnp.sum(hit * weights, axis=0, keepdims=True))
        taken = jnp.concatenate(hits + [jnp.zeros((4, tokens), F32)], axis=0)
        rank = dot(taken.astype(BF16), upper)
        place = lax.broadcasted_iota(jnp.int32, (HEAD, tokens), 0).astype(F32)
        picks, scales = [], []
        for local in range(2):
            chosen, scale = [], None
            for turn in range(2):
                at = turn * 2 + local
                slot = jnp.where(
                    taken[at : at + 1] > 0, rank[at : at + 1] + float(turn * MOST), -1.0
                )
                equal = place == slot
                chosen.append(equal.astype(F32))
                term = jnp.sum(jnp.where(equal, heavy[at], 0.0), axis=1, keepdims=True)
                scale = term if scale is None else scale + term
            picks.append(jnp.concatenate(chosen, axis=1))
            scales.append(scale)
        pick = jnp.concatenate(picks, axis=0).astype(BF16)
        rows = jnp.concatenate(
            [gath[root * 2, 0:tokens, :], gath[root * 2 + 1, 0:tokens, :]], axis=0
        )
        routed = dot(pick, rows)
        return [routed[local * HEAD : (local + 1) * HEAD] * scales[local] for local in range(2)]

    chunks = half // 128
    count = part.shape[2]

    def packed(sums, row, lane):
        def piece(value, first, rows, chunk):
            at = lane + chunk * 128
            return value[row + first : row + first + rows, at : at + 128]

        pieces = [piece(s, 0, 32, chunk) for chunk in range(chunks) for s in sums]
        rest = [piece(s, 32, 8, chunk) for s in sums for chunk in range(chunks)]
        for first in range(0, len(rest), 4):
            tile = rest[first]
            for k, other in enumerate(rest[first + 1 : first + 4]):
                tile = tile + pltpu.roll(other, 2 * k + 2, 0)
            pieces.append(tile)
        spare = count - sum(p.shape[0] for p in pieces)
        if spare:
            pieces.append(jnp.zeros((spare, 128), F32))
        return jnp.concatenate(pieces, axis=0)

    def process(roots):
        found = [rows_of(root) for root in roots]
        sums = []
        for local in range(2):
            lhs = jnp.concatenate([f[local] for f in found], axis=0).astype(BF16)
            sums.append(dot(lhs, w_ref[local], ((1,), (1,))))
        for n, root in enumerate(roots):
            for which in range(2):
                part[root, which] = packed(sums, n * HEAD, which * half).astype(BF16)
            jx, jy = root // side, root % side

            @pl.when(jy != y)
            def _():
                first_a(root).start()

            @pl.when(jx != x)
            def _():
                first_b(root).start()

    def first_a(root):
        jx, jy = root // side, root % side
        off = lax.rem(jy - y + side, side)
        slot = jnp.maximum(off - 1, 0)
        return copy(part.at[root, 0], rxa.at[jx, slot], s_a.at[root], r_a.at[jx, slot], x * side + jy, ex)

    def first_b(root):
        jx, jy = root // side, root % side
        off = lax.rem(jx - x + side, side)
        slot = jnp.maximum(off - 1, 0)
        return copy(part.at[root, 1], rxb.at[jy, slot], s_b.at[root], r_b.at[jy, slot], jx * side + y, ex)

    def arrived(block):
        go_right(block).wait_recv()

    def get(step, on_right=False, on_left=False):
        block = at_z(step)[1]
        arrived(block)
        if on_right:
            go_right(block).start()
        if on_left:
            go_left(block).start()
        go_across(block).start()

    arrived(sibling)
    process([z])
    steps = (
        (1, ((1, False, True), (-1, True, False))),
        (5, ((5, True, True), (-5, True, True))),
        (2, ((2, False, False), (-2, False, False))),
        (4, ((4, True, False), (-6, True, False), (6, False, True), (-4, False, True))),
        (6, ((-7, True, False), (7, False, False))),
        (3, ((3, False, False), (-3, False, False))),
        (7, ((8, False, False),)),
    )

    def ring(turn, carry):
        step = 0
        for n, (away, blocks) in enumerate(steps):
            step = step + jnp.where(turn == n, away, 0)

            @pl.when(turn == n)
            def _():
                for block in blocks:
                    get(*block)

        low, high = at_z(-step)[0], at_z(step)[0]
        arrived(low * 2 + 1 - core)
        arrived(high * 2 + 1 - core)
        process([low, high])
        return carry

    lax.fori_loop(0, len(steps), ring, 0)
    far = at_z(8)[0]
    arrived(far * 2 + 1 - core)
    process([far])

    eye = (
        lax.broadcasted_iota(jnp.int32, (size, PER * size), 0)
        == lax.rem(lax.broadcasted_iota(jnp.int32, (size, PER * size), 1), size)
    ).astype(F32)

    def turn(group, carry):
        mask = maskb[...]
        first = negated_skew(skew_ref[group], maskf[...])
        by_first = both(first, mask)
        second = times(first, by_first)
        series = eye + first
        pair = times(jnp.concatenate([second, series], axis=0), both(second, mask))
        fourth, series = pair[:size], series + pair[size:]
        pair = times(jnp.concatenate([fourth, series], axis=0), both(fourth, mask))
        eighth, series = pair[:size], series + pair[size:]
        series = series + times(series, both(eighth, mask))
        result = series + times(series, by_first)
        rotm[group] = spread(result.astype(BF16), mask)
        return carry

    lax.fori_loop(0, groups, turn, 0)

    def prepare():
        mask = maskb[...]
        given = -negated_skew(skew_ref[jnp.minimum(dp, groups - 1)], maskf[...])

        def keep(which, slab):
            right = both(slab, mask)
            bys[which] = right[0]
            return right

        second = times(given, keep(0, given))
        one = eye + given
        pair = times(jnp.concatenate([second, one], axis=0), keep(1, second))
        fourth, two = pair[:size], one + pair[size:]
        pair = times(jnp.concatenate([fourth, two], axis=0), keep(2, fourth))
        eighth, three = pair[:size], two + pair[size:]
        keep(4, three + times(three, keep(3, eighth)))
        for which, slab in enumerate((given, second, one, fourth, two, three)):
            lefts[which] = slab.astype(BF16)

    prepare()

    def gather_a(jx, carry):
        root = jx * side + y
        total = part[root, 0].astype(F32)
        for slot in range(side - 1):
            copy(part.at[root, 0], rxa.at[jx, slot], s_a.at[root], r_a.at[jx, slot], dp, ex).wait_recv()
            total = total + rxa[jx, slot].astype(F32)
        mida[jx] = total.astype(BF16)

        @pl.when(jx != x)
        def _():
            second_a(jx).start()

        return carry

    def second_a(jx):
        slot = jnp.maximum(lax.rem(jx - x + side, side) - 1, 0)
        return copy(mida.at[jx], tra.at[slot], s_ma.at[jx], r_ma.at[slot], jx * side + y, ex)

    def gather_b(jy, carry):
        root = x * side + jy
        total = part[root, 1].astype(F32)
        for slot in range(side - 1):
            copy(part.at[root, 1], rxb.at[jy, slot], s_b.at[root], r_b.at[jy, slot], dp, ex).wait_recv()
            total = total + rxb[jy, slot].astype(F32)
        midb[jy] = total.astype(BF16)

        @pl.when(jy != y)
        def _():
            second_b(jy).start()

        return carry

    def second_b(jy):
        slot = jnp.maximum(lax.rem(jy - y + side, side) - 1, 0)
        return copy(midb.at[jy], trb.at[slot], s_mb.at[jy], r_mb.at[slot], x * side + jy, ex)

    def gather_both(step, carry):
        gather_a(lax.rem(z // side + step + step // 2 - 2 * (step // 3), side), 0)
        gather_b(lax.rem(y + 1 + step, side), 0)
        return carry

    lax.fori_loop(0, side, gather_both, 0)

    for which, (mid, at, tr, s_m, r_m) in enumerate(((mida, x, tra, s_ma, r_ma), (midb, y, trb, s_mb, r_mb))):
        total = mid[at].astype(F32)
        for slot in range(side - 1):
            copy(mid.at[0], tr.at[slot], s_m.at[0], r_m.at[slot], dp, ex).wait_recv()
            total = total + tr[slot].astype(F32)
        for local in range(2):
            for chunk in range(chunks):
                at = local * chunks + chunk
                start = 64 * chunks + at // 4 * 8
                tile = total[start : start + 8]
                if at % 4:
                    tile = pltpu.roll(tile, 8 - at % 4 * 2, 0)
                tile = jnp.where(lax.broadcasted_iota(jnp.int32, (8, 128), 0) < 2, tile, 0.0)
                start = chunk * 64 + local * 32
                lane = which * half + chunk * 128
                rgs[local, :, lane : lane + 128] = jnp.concatenate(
                    [total[start : start + 32], tile, jnp.zeros((DEEP - HEAD, 128), F32)], axis=0
                ).astype(BF16)

    def lanes_of(group):
        return pl.ds(pl.multiple_of((group % per_expert) * PER * size, PER * size), PER * size)

    def rot_copy(group):
        return copy(rotp.at[group], rotrx.at[dp], s_rot.at[group], r_rot.at[dp], group, ex)

    def grads(step, carry):
        group = lax.rem(dp + 1 + step, groups)
        local, lanes = group // per_expert, lanes_of(group)
        square = dot(act_ref[local, :, lanes], rgs[local, :, lanes], ((0,), (0,)))
        rotp[group] = fold(square * maskf[...]).astype(BF16)

        @pl.when(group != dp)
        def _():
            rot_copy(group).start()

        return carry

    lax.fori_loop(0, groups, grads, 0)

    def hide(group, carry):
        local, lanes = group // per_expert, lanes_of(group)
        hid_ref[local, :, lanes] = dot(rgs[local, :, lanes], rotm[group], ((1,), (1,))).astype(BF16)
        return carry

    lax.fori_loop(0, groups, hide, 0)

    def pull_copy(owner, peer):
        return copy(pull.at[owner], pull.at[owner], s_pull.at[peer], r_pull.at[owner], peer, ex)

    @pl.when(dp < groups)
    def _():
        mask = maskb[...]

        def add(step, total):
            source = lax.rem(dp + step, n_dp)
            copy(rotp.at[0], rotrx.at[source], s_rot.at[0], r_rot.at[source], dp, ex).wait_recv()
            return total + rotrx[source].astype(F32)

        change = lax.fori_loop(1, n_dp, add, rotp[dp].astype(F32))
        change_b = change.astype(BF16)

        none = dp // n_dp

        def put(at, left, right):
            rows = left.shape[0] // size
            values[at : at + rows] = dot(left, right).reshape(rows, size, PER * size)
            return [values[at + row + none] for row in range(rows)]

        def rows_at(first, count):
            return lefts[first : first + count].reshape(count * size, PER * size)

        (front,) = put(0, rows_at(0, 1), spread(change_b, mask))
        (back,) = put(1, change_b, bys[0])
        change2 = (front + back).astype(BF16)
        front, lower = put(2, rows_at(1, 2), spread(change2, mask))
        (back,) = put(4, change2, bys[1])
        change4 = (front + back).astype(BF16)
        (back,) = put(5, change_b, bys[1])
        two_change = change + back + lower
        front, lower = put(6, rows_at(3, 2), spread(change4, mask))
        (back,) = put(8, change4, bys[2])
        change8 = (front + back).astype(BF16)
        (back,) = put(9, two_change.astype(BF16), bys[2])
        three_change = two_change + back + lower
        (lower,) = put(10, rows_at(5, 1), spread(change8, mask))
        (back,) = put(11, three_change.astype(BF16), bys[3])
        four_change = three_change + back + lower
        (front,) = put(12, rows_at(0, 1), spread(four_change.astype(BF16), mask))
        (back,) = put(13, change_b, bys[4])
        result = front + four_change + back
        square = spread(result, maskf[...])
        pull[dp] = fold(square.T - square).astype(BF16)

        def tell(step, carry):
            pull_copy(dp, lax.rem(dp + step, n_dp)).start()
            return carry

        lax.fori_loop(1, n_dp, tell, 0)

    def write(step, carry):
        group = lax.rem(dp + groups - step, groups)

        @pl.when(group != dp)
        def _():
            pull_copy(group, dp).wait_recv()

        skg_ref[group] = -(pull[group].astype(F32).T)
        return carry

    lax.fori_loop(0, groups, write, 0)

    go_far(0).wait_send()
    go_far(1).wait_send()
    for step in (0, 5, -5, -1, 4, -6, -7):
        go_right(at_z(step)[1]).wait_send()
    for step in (0, 5, -5, 1, 6, -4):
        go_left(at_z(step)[1]).wait_send()

    def left_across(chip, carry):
        go_across(chip * 2 + core).wait_send()
        return carry

    lax.fori_loop(0, depth, left_across, 0)

    def left_first(root, carry):
        @pl.when(root % side != y)
        def _():
            first_a(root).wait_send()

        @pl.when(root // side != x)
        def _():
            first_b(root).wait_send()

        return carry

    lax.fori_loop(0, n_dp, left_first, 0)

    def left_second(step, carry):
        @pl.when(step != x)
        def _():
            second_a(step).wait_send()

        @pl.when(step != y)
        def _():
            second_b(step).wait_send()

        return carry

    lax.fori_loop(0, side, left_second, 0)

    def left_rot(group, carry):
        @pl.when(group != dp)
        def _():
            rot_copy(group).wait_send()

        return carry

    lax.fori_loop(0, groups, left_rot, 0)

    @pl.when(dp < groups)
    def _():
        def told(step, carry):
            pull_copy(dp, lax.rem(dp + step, n_dp)).wait_send()
            return carry

        lax.fori_loop(1, n_dp, told, 0)


def body(side, depth, grad_out, route_ids, route_weights, hidden_act, down_weight, skew_param):
    tokens, feat = grad_out.shape
    local, slots_here, hidden = hidden_act.shape
    blocks, size = skew_param.shape[1], skew_param.shape[2]
    groups = local * blocks // PER
    n_dp = side * side
    half = hidden // 2
    wide = PER * size
    chunks = half // 128
    packed = -(-(64 * chunks + (2 * chunks + 3) // 4 * 8) // 16) * 16
    act = jnp.pad(hidden_act, ((0, 0), (0, DEEP - slots_here), (0, 0)))
    vmem = pl.BlockSpec(memory_space=pltpu.VMEM)
    dma = pltpu.SemaphoreType.DMA
    hid, skg = pl.pallas_call(
        functools.partial(kernel, side, depth, groups),
        out_shape=(
            jax.ShapeDtypeStruct((local, DEEP, hidden), BF16),
            jax.ShapeDtypeStruct((groups, wide, size), F32),
        ),
        in_specs=[vmem] * 6,
        out_specs=(vmem, vmem),
        scratch_shapes=[
            pltpu.VMEM((2 * depth, tokens + 16, feat), BF16),
            pltpu.VMEM((n_dp, 2, packed, 128), BF16),
            pltpu.VMEM((side, side - 1, packed, 128), BF16),
            pltpu.VMEM((side, side - 1, packed, 128), BF16),
            pltpu.VMEM((side, packed, 128), BF16),
            pltpu.VMEM((side, packed, 128), BF16),
            pltpu.VMEM((side - 1, packed, 128), BF16),
            pltpu.VMEM((side - 1, packed, 128), BF16),
            pltpu.VMEM((local, DEEP, hidden), BF16),
            pltpu.VMEM((groups, wide, wide), BF16),
            pltpu.VMEM((groups, size, wide), BF16),
            pltpu.VMEM((n_dp, size, wide), BF16),
            pltpu.VMEM((groups, size, wide), BF16),
            pltpu.VMEM((wide, wide), F32),
            pltpu.VMEM((wide, wide), BF16),
            pltpu.VMEM((5, wide, wide), BF16),
            pltpu.VMEM((6, size, wide), BF16),
            pltpu.VMEM((14, size, wide), F32),
            dma((depth,)), dma((depth,)), dma((2,)), dma((depth,)), dma((2 * depth,)),
            dma((n_dp,)), dma((n_dp,)), dma((side, side - 1)), dma((side, side - 1)),
            dma((side,)), dma((side,)), dma((side - 1,)), dma((side - 1,)),
            dma((groups,)), dma((n_dp,)), dma((n_dp,)), dma((groups,)),
        ],
        compiler_params=pltpu.CompilerParams(
            collective_id=0, has_side_effects=True, vmem_limit_bytes=50 * 1024 * 1024
        ),
    )(
        route_ids.T, route_weights.T, grad_out, act, down_weight,
        skew_param.reshape(groups, wide, size),
    )
    return hid[:, :slots_here], skg.reshape(skew_param.shape)


def solution(mesh):
    in_specs = (
        P("expert", "dp"),
        P("expert", None),
        P("expert", None),
        P("expert", "dp", None),
        P("expert", None, "dp"),
        P("expert", None, None, None),
    )
    out_specs = (P("expert", "dp", None), P("expert", None, None, None))
    side = {4: 2, 16: 4}[mesh.shape["dp"]]
    return jax.shard_map(
        functools.partial(body, side, mesh.shape["expert"] // 2),
        mesh=mesh, in_specs=in_specs, out_specs=out_specs, check_vma=False,
    )
```

```python
import functools

import jax
import jax.numpy as jnp
from jax import lax
from jax.experimental import pallas as pl
from jax.experimental.pallas import tpu as pltpu
from jax.sharding import PartitionSpec as P

F32 = jnp.float32
BF16 = jnp.bfloat16
MESH = pl.DeviceIdType.MESH
MOST = 17
PER = 4
HEAD = 40
DEEP = 48


def dot(a, b, dims=((1,), (0,))):
    return lax.dot_general(a, b, (dims, ((), ())), preferred_element_type=F32)


def halves(value):
    high = value.astype(BF16)
    return high, (value - high.astype(F32)).astype(BF16)


def spread(slab, mask):
    return jnp.concatenate([slab] * PER, axis=0) * mask


def fold(square):
    size = square.shape[0] // PER
    total = square[:size]
    for band in range(1, PER):
        total = total + square[band * size : (band + 1) * size]
    return total


def both(slab, mask):
    high, low = halves(slab)
    return spread(high, mask), spread(low, mask)


def times(left, right):
    rows = left.shape[0]
    high, low = halves(left)
    first = dot(jnp.concatenate([high, low], axis=0), right[0])
    return first[:rows] + first[rows:] + dot(high, right[1])


def negated_skew(stack, mask):
    square = spread(stack.T, mask)
    return fold(square - square.T)


def kernel(
    side, depth, groups,
    ids_ref, wts_ref, grad_ref, act_ref, w_ref, skew_ref,
    hid_ref, skg_ref,
    gath, part, rxa, rxb, mida, midb, tra, trb, rgs, rotm, rotp, rotrx, pull, maskf, maskb, bys, lefts, values,
    s_right, s_left, s_far, s_sib, r_gath, s_a, s_b, r_a, r_b, s_ma, s_mb, r_ma, r_mb,
    s_rot, r_rot, s_pull, r_pull,
):
    n_dp = side * side
    dp = lax.axis_index("dp")
    ex = lax.axis_index("expert")
    x, y = dp // side, dp % side
    z, core = ex // 2, ex % 2
    hidden = w_ref.shape[1]
    half = hidden // 2
    size = skew_ref.shape[1] // PER
    per_expert = groups // 2
    jump = 5

    def at_z(step):
        chip = lax.rem(z + step + depth, depth)
        return chip, chip * 2 + core

    right, left = at_z(1)[1], at_z(-1)[1]
    beyond, before = at_z(jump)[1], at_z(-jump)[1]
    sibling = z * 2 + (1 - core)

    def copy(src, dst, send, recv, to_dp, to_ex):
        return pltpu.make_async_remote_copy(
            src_ref=src, dst_ref=dst, send_sem=send, recv_sem=recv,
            device_id=(to_dp, to_ex), device_id_type=MESH,
        )

    barrier = pltpu.get_barrier_semaphore()
    for peer in (right, left, beyond, before, sibling):
        pl.semaphore_signal(barrier, inc=1, device_id=(dp, peer), device_id_type=MESH)

    def greet(step, carry):
        pl.semaphore_signal(
            barrier, inc=1, device_id=(lax.rem(dp + step, n_dp), ex), device_id_type=MESH
        )
        return carry

    lax.fori_loop(1, n_dp, greet, 0)

    tokens = grad_ref.shape[0]
    own = ex
    gath[own, 0:tokens, :] = grad_ref[...]
    weight = wts_ref[...]
    w1 = weight.astype(BF16).astype(F32)
    w2 = (weight - w1).astype(BF16).astype(F32)
    w3 = weight - w1 - w2
    info = jnp.concatenate(
        [
            jnp.concatenate([ids_ref[...].astype(F32), w1], axis=1),
            jnp.concatenate([w2, w3], axis=1),
        ],
        axis=0,
    )
    gath[own, tokens : tokens + 16, :] = info.astype(BF16)

    row_i = lax.broadcasted_iota(jnp.int32, (PER * size, PER * size), 0) // size
    col_i = lax.broadcasted_iota(jnp.int32, (PER * size, PER * size), 1) // size
    maskf[...] = (row_i == col_i).astype(F32)
    maskb[...] = (row_i == col_i).astype(F32).astype(BF16)

    pl.semaphore_wait(barrier, n_dp - 1 + 5)

    def go_right(block):
        return copy(gath.at[block], gath.at[block], s_right.at[block // 2], r_gath.at[block], dp, right)

    def go_left(block):
        return copy(gath.at[block], gath.at[block], s_left.at[block // 2], r_gath.at[block], dp, left)

    def go_across(block):
        return copy(gath.at[block], gath.at[block], s_sib.at[block // 2], r_gath.at[block], dp, sibling)

    def go_far(n):
        return copy(
            gath.at[own], gath.at[own], s_far.at[n], r_gath.at[own], dp, (beyond, before)[n]
        )

    go_far(0).start()
    go_far(1).start()
    go_right(own).start()
    go_left(own).start()
    go_across(own).start()

    upper = (
        lax.broadcasted_iota(jnp.int32, (tokens, tokens), 0)
        < lax.broadcasted_iota(jnp.int32, (tokens, tokens), 1)
    ).astype(F32).astype(BF16)

    def rows_of(root):
        hits, heavy = [], []
        for turn in range(2):
            data = gath[root * 2 + turn, tokens : tokens + 16, :].astype(F32)
            named = data[0:8, 0:tokens]
            weights = data[0:8, tokens:] + data[8:16, 0:tokens] + data[8:16, tokens:]
            for local in range(2):
                hit = (named == (ex * 2 + local).astype(F32)).astype(F32)
                hits.append(jnp.sum(hit, axis=0, keepdims=True))
                heavy.append(jnp.sum(hit * weights, axis=0, keepdims=True))
        taken = jnp.concatenate(hits + [jnp.zeros((4, tokens), F32)], axis=0)
        rank = dot(taken.astype(BF16), upper)
        place = lax.broadcasted_iota(jnp.int32, (HEAD, tokens), 0).astype(F32)
        picks, scales = [], []
        for local in range(2):
            chosen, scale = [], None
            for turn in range(2):
                at = turn * 2 + local
                slot = jnp.where(
                    taken[at : at + 1] > 0, rank[at : at + 1] + float(turn * MOST), -1.0
                )
                equal = place == slot
                chosen.append(equal.astype(F32))
                term = jnp.sum(jnp.where(equal, heavy[at], 0.0), axis=1, keepdims=True)
                scale = term if scale is None else scale + term
            picks.append(jnp.concatenate(chosen, axis=1))
            scales.append(scale)
        pick = jnp.concatenate(picks, axis=0).astype(BF16)
        rows = jnp.concatenate(
            [gath[root * 2, 0:tokens, :], gath[root * 2 + 1, 0:tokens, :]], axis=0
        )
        routed = dot(pick, rows)
        return [routed[local * HEAD : (local + 1) * HEAD] * scales[local] for local in range(2)]

    chunks = half // 128
    count = part.shape[2]

    def packed(sums, row, lane):
        def piece(value, first, rows, chunk):
            at = lane + chunk * 128
            return value[row + first : row + first + rows, at : at + 128]

        pieces = [piece(s, 0, 32, chunk) for chunk in range(chunks) for s in sums]
        rest = [piece(s, 32, 8, chunk) for s in sums for chunk in range(chunks)]
        for first in range(0, len(rest), 4):
            tile = rest[first]
            for k, other in enumerate(rest[first + 1 : first + 4]):
                tile = tile + pltpu.roll(other, 2 * k + 2, 0)
            pieces.append(tile)
        spare = count - sum(p.shape[0] for p in pieces)
        if spare:
            pieces.append(jnp.zeros((spare, 128), F32))
        return jnp.concatenate(pieces, axis=0)

    def process(roots):
        found = [rows_of(root) for root in roots]
        sums = []
        for local in range(2):
            lhs = jnp.concatenate([f[local] for f in found], axis=0).astype(BF16)
            sums.append(dot(lhs, w_ref[local], ((1,), (1,))))
        for n, root in enumerate(roots):
            for which in range(2):
                part[root, which] = packed(sums, n * HEAD, which * half).astype(BF16)
            jx, jy = root // side, root % side

            @pl.when(jy != y)
            def _():
                first_a(root).start()

            @pl.when(jx != x)
            def _():
                first_b(root).start()

    def first_a(root):
        jx, jy = root // side, root % side
        off = lax.rem(jy - y + side, side)
        slot = jnp.maximum(off - 1, 0)
        return copy(part.at[root, 0], rxa.at[jx, slot], s_a.at[root], r_a.at[jx, slot], x * side + jy, ex)

    def first_b(root):
        jx, jy = root // side, root % side
        off = lax.rem(jx - x + side, side)
        slot = jnp.maximum(off - 1, 0)
        return copy(part.at[root, 1], rxb.at[jy, slot], s_b.at[root], r_b.at[jy, slot], jx * side + y, ex)

    def arrived(block):
        go_right(block).wait_recv()

    def get(step, on_right=False, on_left=False):
        block = at_z(step)[1]
        arrived(block)
        if on_right:
            go_right(block).start()
        if on_left:
            go_left(block).start()
        go_across(block).start()

    arrived(sibling)
    process([z])
    steps = (
        (1, ((1, False, True), (-1, True, False))),
        (5, ((5, True, True), (-5, True, True))),
        (2, ((2, False, False), (-2, False, False))),
        (4, ((4, True, False), (-6, True, False), (6, False, True), (-4, False, True))),
        (6, ((-7, True, False), (7, False, False))),
        (3, ((3, False, False), (-3, False, False))),
        (7, ((8, False, False),)),
    )

    def ring(turn, carry):
        step = 0
        for n, (away, blocks) in enumerate(steps):
            step = step + jnp.where(turn == n, away, 0)

            @pl.when(turn == n)
            def _():
                for block in blocks:
                    get(*block)

        low, high = at_z(-step)[0], at_z(step)[0]
        arrived(low * 2 + 1 - core)
        arrived(high * 2 + 1 - core)
        process([low, high])
        return carry

    lax.fori_loop(0, len(steps), ring, 0)
    far = at_z(8)[0]
    arrived(far * 2 + 1 - core)
    process([far])

    eye = (
        lax.broadcasted_iota(jnp.int32, (size, PER * size), 0)
        == lax.rem(lax.broadcasted_iota(jnp.int32, (size, PER * size), 1), size)
    ).astype(F32)

    def turn(group, carry):
        mask = maskb[...]
        first = negated_skew(skew_ref[group], maskf[...])
        by_first = both(first, mask)
        second = times(first, by_first)
        series = eye + first
        pair = times(jnp.concatenate([second, series], axis=0), both(second, mask))
        fourth, series = pair[:size], series + pair[size:]
        pair = times(jnp.concatenate([fourth, series], axis=0), both(fourth, mask))
        eighth, series = pair[:size], series + pair[size:]
        series = series + times(series, both(eighth, mask))
        result = series + times(series, by_first)
        rotm[group] = spread(result.astype(BF16), mask)
        return carry

    lax.fori_loop(0, groups, turn, 0)

    def prepare():
        mask = maskb[...]
        given = -negated_skew(skew_ref[jnp.minimum(dp, groups - 1)], maskf[...])

        def keep(which, slab):
            right = both(slab, mask)
            bys[which] = right[0]
            return right

        second = times(given, keep(0, given))
        one = eye + given
        pair = times(jnp.concatenate([second, one], axis=0), keep(1, second))
        fourth, two = pair[:size], one + pair[size:]
        pair = times(jnp.concatenate([fourth, two], axis=0), keep(2, fourth))
        eighth, three = pair[:size], two + pair[size:]
        keep(4, three + times(three, keep(3, eighth)))
        for which, slab in enumerate((given, second, one, fourth, two, three)):
            lefts[which] = slab.astype(BF16)

    prepare()

    def gather_a(jx, carry):
        root = jx * side + y
        total = part[root, 0].astype(F32)
        for slot in range(side - 1):
            copy(part.at[root, 0], rxa.at[jx, slot], s_a.at[root], r_a.at[jx, slot], dp, ex).wait_recv()
            total = total + rxa[jx, slot].astype(F32)
        mida[jx] = total.astype(BF16)

        @pl.when(jx != x)
        def _():
            second_a(jx).start()

        return carry

    def second_a(jx):
        slot = jnp.maximum(lax.rem(jx - x + side, side) - 1, 0)
        return copy(mida.at[jx], tra.at[slot], s_ma.at[jx], r_ma.at[slot], jx * side + y, ex)

    def gather_b(jy, carry):
        root = x * side + jy
        total = part[root, 1].astype(F32)
        for slot in range(side - 1):
            copy(part.at[root, 1], rxb.at[jy, slot], s_b.at[root], r_b.at[jy, slot], dp, ex).wait_recv()
            total = total + rxb[jy, slot].astype(F32)
        midb[jy] = total.astype(BF16)

        @pl.when(jy != y)
        def _():
            second_b(jy).start()

        return carry

    def second_b(jy):
        slot = jnp.maximum(lax.rem(jy - y + side, side) - 1, 0)
        return copy(midb.at[jy], trb.at[slot], s_mb.at[jy], r_mb.at[slot], x * side + jy, ex)

    def gather_both(step, carry):
        gather_a(lax.rem(z // side + step + step // 2 - 2 * (step // 3), side), 0)
        gather_b(lax.rem(y + 1 + step, side), 0)
        return carry

    lax.fori_loop(0, side, gather_both, 0)

    for which, (mid, at, tr, s_m, r_m) in enumerate(((mida, x, tra, s_ma, r_ma), (midb, y, trb, s_mb, r_mb))):
        total = mid[at].astype(F32)
        for slot in range(side - 1):
            copy(mid.at[0], tr.at[slot], s_m.at[0], r_m.at[slot], dp, ex).wait_recv()
            total = total + tr[slot].astype(F32)
        for local in range(2):
            for chunk in range(chunks):
                at = local * chunks + chunk
                start = 64 * chunks + at // 4 * 8
                tile = total[start : start + 8]
                if at % 4:
                    tile = pltpu.roll(tile, 8 - at % 4 * 2, 0)
                tile = jnp.where(lax.broadcasted_iota(jnp.int32, (8, 128), 0) < 2, tile, 0.0)
                start = chunk * 64 + local * 32
                lane = which * half + chunk * 128
                rgs[local, :, lane : lane + 128] = jnp.concatenate(
                    [total[start : start + 32], tile, jnp.zeros((DEEP - HEAD, 128), F32)], axis=0
                ).astype(BF16)

    def lanes_of(group):
        return pl.ds(pl.multiple_of((group % per_expert) * PER * size, PER * size), PER * size)

    def rot_copy(group):
        return copy(rotp.at[group], rotrx.at[dp], s_rot.at[group], r_rot.at[dp], group, ex)

    def grads(step, carry):
        group = lax.rem(dp + 1 + step, groups)
        local, lanes = group // per_expert, lanes_of(group)
        square = dot(act_ref[local, :, lanes], rgs[local, :, lanes], ((0,), (0,)))
        rotp[group] = fold(square * maskf[...]).astype(BF16)

        @pl.when(group != dp)
        def _():
            rot_copy(group).start()

        return carry

    lax.fori_loop(0, groups, grads, 0)

    def hide(group, carry):
        local, lanes = group // per_expert, lanes_of(group)
        hid_ref[local, :, lanes] = dot(rgs[local, :, lanes], rotm[group], ((1,), (1,))).astype(BF16)
        return carry

    lax.fori_loop(0, groups, hide, 0)

    def above(sign):
        shape = (size, PER * size // 2)
        row = lax.broadcasted_iota(jnp.int32, shape, 0)
        return sign * (lax.rem(lax.broadcasted_iota(jnp.int32, shape, 1), size) - row) > 0

    def pull_copy(owner, peer):
        return copy(pull.at[owner], pull.at[owner], s_pull.at[peer], r_pull.at[owner], peer, ex)

    @pl.when(dp < groups)
    def _():
        mask = maskb[...]

        def add(step, total):
            source = lax.rem(dp + step, n_dp)
            copy(rotp.at[0], rotrx.at[source], s_rot.at[0], r_rot.at[source], dp, ex).wait_recv()
            return total + rotrx[source].astype(F32)

        change = lax.fori_loop(1, n_dp, add, rotp[dp].astype(F32))
        change_b = change.astype(BF16)

        none = dp // n_dp

        def put(at, left, right):
            rows = left.shape[0] // size
            values[at : at + rows] = dot(left, right).reshape(rows, size, PER * size)
            return [values[at + row + none] for row in range(rows)]

        def rows_at(first, count):
            return lefts[first : first + count].reshape(count * size, PER * size)

        (front,) = put(0, rows_at(0, 1), spread(change_b, mask))
        (back,) = put(1, change_b, bys[0])
        change2 = (front + back).astype(BF16)
        front, lower = put(2, rows_at(1, 2), spread(change2, mask))
        (back,) = put(4, change2, bys[1])
        change4 = (front + back).astype(BF16)
        (back,) = put(5, change_b, bys[1])
        two_change = change + back + lower
        front, lower = put(6, rows_at(3, 2), spread(change4, mask))
        (back,) = put(8, change4, bys[2])
        change8 = (front + back).astype(BF16)
        (back,) = put(9, two_change.astype(BF16), bys[2])
        three_change = two_change + back + lower
        (lower,) = put(10, rows_at(5, 1), spread(change8, mask))
        (back,) = put(11, three_change.astype(BF16), bys[3])
        four_change = three_change + back + lower
        (front,) = put(12, rows_at(0, 1), spread(four_change.astype(BF16), mask))
        (back,) = put(13, change_b, bys[4])
        result = front + four_change + back
        square = spread(result, maskf[...])
        slab = fold(square.T - square)
        wide = PER * size // 2
        pull[dp] = jnp.where(
            above(1), slab[:, :wide], jnp.where(above(-1), slab[:, wide:], 0.0)
        ).astype(BF16)

        def tell(step, carry):
            pull_copy(dp, lax.rem(dp + step, n_dp)).start()
            return carry

        lax.fori_loop(1, n_dp, tell, 0)

    def write(step, carry):
        group = lax.rem(dp + groups - step, groups)

        @pl.when(group != dp)
        def _():
            pull_copy(group, dp).wait_recv()

        given = pull[group].astype(F32)
        for n, sign in enumerate((1, -1)):
            part_of = jnp.where(above(sign), given, 0.0)
            stacked = jnp.concatenate([part_of[:, :size], part_of[:, size:]], axis=0)
            skg_ref[group, n * 2 * size : (n + 1) * 2 * size, :] = stacked - part_of.T
        return carry

    lax.fori_loop(0, groups, write, 0)

    go_far(0).wait_send()
    go_far(1).wait_send()
    for step in (0, 5, -5, -1, 4, -6, -7):
        go_right(at_z(step)[1]).wait_send()
    for step in (0, 5, -5, 1, 6, -4):
        go_left(at_z(step)[1]).wait_send()

    def left_across(chip, carry):
        go_across(chip * 2 + core).wait_send()
        return carry

    lax.fori_loop(0, depth, left_across, 0)

    def left_first(root, carry):
        @pl.when(root % side != y)
        def _():
            first_a(root).wait_send()

        @pl.when(root // side != x)
        def _():
            first_b(root).wait_send()

        return carry

    lax.fori_loop(0, n_dp, left_first, 0)

    def left_second(step, carry):
        @pl.when(step != x)
        def _():
            second_a(step).wait_send()

        @pl.when(step != y)
        def _():
            second_b(step).wait_send()

        return carry

    lax.fori_loop(0, side, left_second, 0)

    def left_rot(group, carry):
        @pl.when(group != dp)
        def _():
            rot_copy(group).wait_send()

        return carry

    lax.fori_loop(0, groups, left_rot, 0)

    @pl.when(dp < groups)
    def _():
        def told(step, carry):
            pull_copy(dp, lax.rem(dp + step, n_dp)).wait_send()
            return carry

        lax.fori_loop(1, n_dp, told, 0)


def body(side, depth, grad_out, route_ids, route_weights, hidden_act, down_weight, skew_param):
    tokens, feat = grad_out.shape
    local, slots_here, hidden = hidden_act.shape
    blocks, size = skew_param.shape[1], skew_param.shape[2]
    groups = local * blocks // PER
    n_dp = side * side
    half = hidden // 2
    wide = PER * size
    chunks = half // 128
    packed = -(-(64 * chunks + (2 * chunks + 3) // 4 * 8) // 16) * 16
    act = jnp.pad(hidden_act, ((0, 0), (0, DEEP - slots_here), (0, 0)))
    vmem = pl.BlockSpec(memory_space=pltpu.VMEM)
    dma = pltpu.SemaphoreType.DMA
    hid, skg = pl.pallas_call(
        functools.partial(kernel, side, depth, groups),
        out_shape=(
            jax.ShapeDtypeStruct((local, DEEP, hidden), BF16),
            jax.ShapeDtypeStruct((groups, wide, size), F32),
        ),
        in_specs=[vmem] * 6,
        out_specs=(vmem, vmem),
        scratch_shapes=[
            pltpu.VMEM((2 * depth, tokens + 16, feat), BF16),
            pltpu.VMEM((n_dp, 2, packed, 128), BF16),
            pltpu.VMEM((side, side - 1, packed, 128), BF16),
            pltpu.VMEM((side, side - 1, packed, 128), BF16),
            pltpu.VMEM((side, packed, 128), BF16),
            pltpu.VMEM((side, packed, 128), BF16),
            pltpu.VMEM((side - 1, packed, 128), BF16),
            pltpu.VMEM((side - 1, packed, 128), BF16),
            pltpu.VMEM((local, DEEP, hidden), BF16),
            pltpu.VMEM((groups, wide, wide), BF16),
            pltpu.VMEM((groups, size, wide), BF16),
            pltpu.VMEM((n_dp, size, wide), BF16),
            pltpu.VMEM((groups, size, wide // 2), BF16),
            pltpu.VMEM((wide, wide), F32),
            pltpu.VMEM((wide, wide), BF16),
            pltpu.VMEM((5, wide, wide), BF16),
            pltpu.VMEM((6, size, wide), BF16),
            pltpu.VMEM((14, size, wide), F32),
            dma((depth,)), dma((depth,)), dma((2,)), dma((depth,)), dma((2 * depth,)),
            dma((n_dp,)), dma((n_dp,)), dma((side, side - 1)), dma((side, side - 1)),
            dma((side,)), dma((side,)), dma((side - 1,)), dma((side - 1,)),
            dma((groups,)), dma((n_dp,)), dma((n_dp,)), dma((groups,)),
        ],
        compiler_params=pltpu.CompilerParams(
            collective_id=0, has_side_effects=True, vmem_limit_bytes=50 * 1024 * 1024
        ),
    )(
        route_ids.T, route_weights.T, grad_out, act, down_weight,
        skew_param.reshape(groups, wide, size),
    )
    return hid[:, :slots_here], skg.reshape(skew_param.shape)


def solution(mesh):
    in_specs = (
        P("expert", "dp"),
        P("expert", None),
        P("expert", None),
        P("expert", "dp", None),
        P("expert", None, "dp"),
        P("expert", None, None, None),
    )
    out_specs = (P("expert", "dp", None), P("expert", None, None, None))
    side = {4: 2, 16: 4}[mesh.shape["dp"]]
    return jax.shard_map(
        functools.partial(body, side, mesh.shape["expert"] // 2),
        mesh=mesh, in_specs=in_specs, out_specs=out_specs, check_vma=False,
    )
```
